32 devices in a mesh: seq: 8 (over z, x), grp: 4 (over y, core).
Axes of the slice: x: 2, y: 2, z: 4, core: 2. Of those that a mesh axis runs over, the one named last changes fastest.
Arguments:
- query_rows: bfloat16 [32768, 2048], P(('seq', 'grp')), may hold values from -8 to 8
- key_rows: bfloat16 [32768, 2048], P(('seq', 'grp')), may hold values from -8 to 8
- value_rows: bfloat16 [32768, 2048], P(('seq', 'grp')), may hold values from -6 to 6
- cluster_ids: int32 [8, 32768], P(None, ('seq', 'grp')), may hold values from 0 to 255, as said below
Outputs:
- attended: bfloat16 [32768, 2048], P(('seq', 'grp'))
The draws below stay inside these ranges and needn't reach their ends.
Inputs may be any that keep to these rules, and one draw needn't show every extreme that they name: `cluster_ids`: in each routed head no cluster is named by more than 6 of one device's 1024 tokens, and in each routed head one cluster is named by exactly 6 tokens of every device.
All inputs are finite; a program needn't handle non-finite values.
Results may differ from the reference program's by a relative error of at most 0.0039.
Values may be sent and summed in bfloat16 or wider, within the bound.
No kernel may reach another device: no remote copies, remote signals or barrier semaphores. Data moves between devices by JAX's collectives and lax.ppermute only.
A program may use at most 192 MiB of HBM per device.

```python
import jax
import jax.numpy as jnp
from jax import lax

HEADS_L = 8
HEADS_R = 8
HEAD_DIM = 128
WINDOW = 1024
CLUSTERS = 256
TOK_DEV = 1024
CAP = 6
TOKENS = 32768


def draw_query_rows(key, part):
    feat_width = (HEADS_L + HEADS_R) * HEAD_DIM
    noise_part = jax.random.normal(jax.random.fold_in(key, 11), (TOKENS, feat_width), jnp.float32)
    field = noise_part
    return jnp.clip(field, -8.0, 8.0).astype(jnp.bfloat16)


def draw_key_rows(key, part):
    feat_width = (HEADS_L + HEADS_R) * HEAD_DIM
    noise_part = jax.random.normal(jax.random.fold_in(key, 21), (TOKENS, feat_width), jnp.float32)
    field = noise_part
    return jnp.clip(field, -8.0, 8.0).astype(jnp.bfloat16)


def draw_cluster_ids(key, part):
    device_count = TOKENS // TOK_DEV
    pool_size = (CLUSTERS - 1) * CAP
    keep_count = TOK_DEV - CAP
    hottest = jax.random.randint(jax.random.fold_in(key, 31), (HEADS_R,), 0, CLUSTERS)
    levels = jax.random.randint(jax.random.fold_in(key, 32), (HEADS_R, CLUSTERS - 1), 0, 4)

    def one_block(flat_index):
        head_index = flat_index // device_count
        block_key = jax.random.fold_in(jax.random.fold_in(key, 33), flat_index)
        noise_part = jax.random.randint(jax.random.fold_in(block_key, 1), (pool_size,), 0, 4096)
        slot_index = jnp.arange(pool_size, dtype=jnp.int32)
        cluster_rank = slot_index // CAP
        priority = (noise_part + levels[head_index][cluster_rank] * 1024) * pool_size + slot_index
        unused, chosen = lax.top_k(priority, keep_count)
        picked = chosen // CAP
        picked = picked + (picked >= hottest[head_index]).astype(jnp.int32)
        filled = jnp.concatenate([picked, jnp.full((CAP,), hottest[head_index], jnp.int32)])
        shuffle = jax.random.permutation(jax.random.fold_in(block_key, 2), TOK_DEV)
        return filled[shuffle]
    blocks = lax.map(one_block, jnp.arange(HEADS_R * device_count, dtype=jnp.int32))
    return blocks.reshape(HEADS_R, TOKENS).astype(jnp.int32)


def block_levels(rng, dims, pieces, least, high):
    loudness = 1.0
    for position, blocks in pieces:
        heights = jax.random.uniform(jax.random.fold_in(jax.random.fold_in(rng, 6), position), (blocks,), jnp.float32, least / len(pieces), high / len(pieces))
        loudness = loudness * jnp.repeat(jnp.exp(heights), dims[position] // blocks).reshape((-1,) + (1,) * (len(dims) - 1 - position))
    return loudness


def bell_draw(key, shape, scale, limit, shards=(), kind=jnp.bfloat16):
    entries = scale * jax.random.normal(key, shape, jnp.float32)
    if shards:
        entries = entries * block_levels(key, shape, shards, -0.22, 0.18)
    return jnp.clip(entries, -limit, limit).astype(kind)


def setup_inputs(seed: int = 0) -> dict:
    seeds = jax.random.split(jax.random.key(seed), 5)
    query_rows = draw_query_rows(jax.random.fold_in(seeds[4], 71), 0)
    key_rows = draw_key_rows(jax.random.fold_in(seeds[4], 71), 0)
    value_rows = bell_draw(seeds[2], (TOKENS, (HEADS_L + HEADS_R) * HEAD_DIM), 1.0, 6.0, ((0, 32),))
    cluster_ids = draw_cluster_ids(jax.random.fold_in(seeds[4], 71), 0)
    return {"query_rows": query_rows, "key_rows": key_rows, "value_rows": value_rows, "cluster_ids": cluster_ids}


NEGATIVE = -1.0e30


def softmax_apply(scores, allowed, value_part):
    masked = jnp.where(allowed, scores, NEGATIVE)
    peak_val = jnp.max(masked, axis=-1, keepdims=True)
    weights = jnp.exp(masked - peak_val)
    totals = jnp.sum(weights, axis=-1, keepdims=True)
    rounded = lax.optimization_barrier(weights.astype(jnp.bfloat16))
    mixture = jnp.einsum("...qk,...kd->...qd", rounded.astype(jnp.float32), value_part.astype(jnp.float32))
    return (mixture / totals).astype(jnp.bfloat16)


def local_heads(query_rows, key_rows, value_rows):
    length = query_rows.shape[0]
    feat_width = HEADS_L * HEAD_DIM
    score_scale = HEAD_DIM ** -0.5
    queries = query_rows[:, :feat_width].reshape(length, HEADS_L, HEAD_DIM)
    padding = jnp.zeros((WINDOW, HEADS_L, HEAD_DIM), query_rows.dtype)
    keys_all = jnp.concatenate([padding, key_rows[:, :feat_width].reshape(length, HEADS_L, HEAD_DIM)], axis=0)
    values_all = jnp.concatenate([padding, value_rows[:, :feat_width].reshape(length, HEADS_L, HEAD_DIM)], axis=0)
    span_rows = TOK_DEV

    def one_block(block_index):
        first_row = (block_index * span_rows).astype(jnp.int32)
        query_blk = lax.dynamic_slice_in_dim(queries, first_row, span_rows, 0)
        key_blk = lax.dynamic_slice_in_dim(keys_all, first_row, span_rows + WINDOW, 0)
        value_blk = lax.dynamic_slice_in_dim(values_all, first_row, span_rows + WINDOW, 0)
        scores = jnp.einsum("qhd,khd->hqk", query_blk.astype(jnp.float32), key_blk.astype(jnp.float32)) * score_scale
        row_ids = jnp.arange(span_rows, dtype=jnp.int32)[:, None]
        col_ids = jnp.arange(span_rows + WINDOW, dtype=jnp.int32)[None, :]
        offset = WINDOW + row_ids - col_ids
        allowed = (offset >= 0) & (offset < WINDOW) & (first_row + col_ids - WINDOW >= 0)
        result = softmax_apply(scores, allowed[None], jnp.transpose(value_blk, (1, 0, 2)))
        return jnp.transpose(result, (1, 0, 2)).reshape(span_rows, feat_width)

    blocks = lax.map(one_block, jnp.arange(length // span_rows, dtype=jnp.int32))
    return blocks.reshape(length, feat_width)


def block_rank(block_ids):
    length = block_ids.shape[0]
    row_ids = jnp.arange(length, dtype=jnp.int32)[:, None]
    col_ids = jnp.arange(length, dtype=jnp.int32)[None, :]
    earlier_same = (block_ids[:, None] == block_ids[None, :]) & (col_ids < row_ids)
    return jnp.sum(earlier_same, axis=1, dtype=jnp.int32)


def routed_head(head_inputs):
    queries, keys_head, values_head, head_ids = head_inputs
    length = head_ids.shape[0]
    device_count = length // TOK_DEV
    slot_total = device_count * CAP
    score_scale = HEAD_DIM ** -0.5
    slot_rank = lax.map(block_rank, head_ids.reshape(device_count, TOK_DEV)).reshape(length)
    source = jnp.arange(length, dtype=jnp.int32) // TOK_DEV
    place = head_ids * slot_total + source * CAP + slot_rank
    table = jnp.full((CLUSTERS * slot_total,), -1, jnp.int32).at[place].set(jnp.arange(length, dtype=jnp.int32))

    def one_cluster(members):
        valid = members >= 0
        safe_ids = jnp.where(valid, members, 0)
        query_part = queries[safe_ids]
        key_part = keys_head[safe_ids]
        value_part = values_head[safe_ids]
        scores = jnp.dot(query_part.astype(jnp.float32), key_part.astype(jnp.float32).T, preferred_element_type=jnp.float32) * score_scale
        allowed = valid[None, :] & (members[None, :] <= members[:, None])
        return softmax_apply(scores, allowed, value_part)

    outputs = lax.map(one_cluster, table.reshape(CLUSTERS, slot_total))
    return outputs.reshape(CLUSTERS * slot_total, HEAD_DIM)[place]


def reference(query_rows, key_rows, value_rows, cluster_ids):
    length = query_rows.shape[0]
    feat_width = HEADS_L * HEAD_DIM
    local_out = local_heads(query_rows, key_rows, value_rows)

    def heads_first(matrix):
        return jnp.transpose(matrix[:, feat_width:].reshape(length, HEADS_R, HEAD_DIM), (1, 0, 2))

    routed = lax.map(routed_head, (heads_first(query_rows), heads_first(key_rows), heads_first(value_rows), cluster_ids))
    routed_out = jnp.transpose(routed, (1, 0, 2)).reshape(length, HEADS_R * HEAD_DIM)
    return jnp.concatenate([local_out, routed_out], axis=1)
```

```python
import functools

import jax
import jax.numpy as jnp
from jax import lax
from jax.experimental import pallas as pl
from jax.experimental.pallas import tpu as pltpu
from jax.sharding import PartitionSpec as P

HEADS_L = 8
HEADS_R = 8
HEAD_DIM = 128
WINDOW = 1024
CLUSTERS = 256

RANKS = 8
NEGATIVE = -1e30
AXES = ("seq", "grp")
SCALE = HEAD_DIM ** (-0.5) * 1.4426950408889634
STAT_ROWS = 32
VMEM = 56 * 1024 * 1024


def params(**extra):
    return pltpu.CompilerParams(vmem_limit_bytes=VMEM, **extra)


def contract_last(a, b):
    return lax.dot_general(a, b, (((1,), (1,)), ((), ())), preferred_element_type=jnp.float32)


def iota(shape, dim):
    return lax.broadcasted_iota(jnp.int32, shape, dim)


def as_mask(condition):
    return jnp.where(condition, 1.0, 0.0).astype(jnp.bfloat16)


def rank_kernel(ids_ref, slot_ref, count_ref):
    heads, rows = ids_ref.shape
    before = as_mask(iota((rows, rows), 0) < iota((rows, rows), 1))
    ones = jnp.ones((8, rows), jnp.bfloat16)
    for head in range(heads):
        ids = ids_ref[head : head + 1, :]
        members = as_mask(iota((CLUSTERS, rows), 0) == ids)
        earlier = jnp.dot(members, before, preferred_element_type=jnp.float32)
        rank = jnp.sum(members.astype(jnp.float32) * earlier, axis=0, keepdims=True)
        slot_ref[head : head + 1, :] = ids * RANKS + rank.astype(jnp.int32)
        count_ref[head : head + 1, :] = contract_last(ones, members)[0:1].astype(jnp.int32)


def rank_tokens(cluster_ids):
    heads, rows = cluster_ids.shape
    return pl.pallas_call(
        rank_kernel,
        out_shape=(
            jax.ShapeDtypeStruct((heads, rows), jnp.int32),
            jax.ShapeDtypeStruct((heads, CLUSTERS), jnp.int32),
        ),
        compiler_params=params(),
        name="rank_tokens",
    )(cluster_ids)


def dispatch_kernel(count, slot_ref, *refs):
    sources, outs = refs[:count], refs[count:]
    rows = slot_ref.shape[-1]
    step = 256
    lines = iota((step, rows), 0)

    def body(part, carry):
        base = part * step
        halves = []
        for side in range(2):
            picks = as_mask(lines == slot_ref[0, side : side + 1, :] - base)
            block = jnp.concatenate(
                [s[side].reshape(rows, HEAD_DIM) for s in sources], axis=1
            )
            found = jnp.dot(picks, block, preferred_element_type=jnp.float32)
            halves.append(found.reshape(step // RANKS, RANKS, count * HEAD_DIM))
        joined = jnp.concatenate(halves, axis=1).astype(jnp.bfloat16)
        for i, out in enumerate(outs):
            out[pl.ds(part * (step // RANKS), step // RANKS), 0] = joined[
                :, :, i * HEAD_DIM : (i + 1) * HEAD_DIM
            ]
        return carry

    lax.fori_loop(0, CLUSTERS * RANKS // step, body, 0)


def dispatch(slots, arrays, name):
    devices, rows = slots.shape
    pairs = devices // 2
    in_specs = [pl.BlockSpec((1, 2, rows), lambda i: (i, 0, 0))]
    operands = [slots.reshape(pairs, 2, rows)]
    for array, part in arrays:
        if part is None:
            in_specs.append(pl.BlockSpec((2, rows, HEAD_DIM), lambda i: (i, 0, 0)))
        else:
            in_specs.append(
                pl.BlockSpec((2, 1, rows, HEAD_DIM), lambda i, part=part: (i, part, 0, 0))
            )
        operands.append(array)
    count = len(arrays)
    shape = (CLUSTERS, pairs, 2 * RANKS, HEAD_DIM)
    flops = 2 * devices * rows * CLUSTERS * RANKS * HEAD_DIM * count
    return pl.pallas_call(
        functools.partial(dispatch_kernel, count),
        grid=(pairs,),
        in_specs=in_specs,
        out_specs=[pl.BlockSpec((CLUSTERS, 1, 2 * RANKS, HEAD_DIM), lambda i: (0, i, 0, 0))]
        * count,
        out_shape=[jax.ShapeDtypeStruct(shape, jnp.bfloat16)] * count,
        compiler_params=params(),
        cost_estimate=pl.CostEstimate(
            flops=flops, bytes_accessed=12_000_000 * count, transcendentals=0
        ),
        name=name,
    )(*operands)


def attend_kernel(count, own, bias_ref, own_k, own_v, pair_k, pair_v, *refs):
    queries, outs = refs[:count], refs[count:]
    block, pairs, lines, width = own_k.shape
    slots = pairs * lines
    lane = iota((slots, 2 * slots), 1)
    row = iota((slots, 2 * slots), 0)
    causal = jnp.where((lane <= row) | (lane >= slots), 0.0, NEGATIVE)
    free = jnp.zeros((slots, 2 * slots), jnp.float32)
    causal = jnp.concatenate([causal if own else free] + [free] * (count - 1), axis=0)
    lane = iota((count * slots, 128), 1)

    def read(ref, c):
        return ref[c].reshape(slots, width)

    def one(c):
        keys = jnp.concatenate([read(own_k, c), read(pair_k, c)], axis=0)
        values = jnp.concatenate([read(own_v, c), read(pair_v, c)], axis=0)
        query = jnp.concatenate([read(q, c) for q in queries], axis=0)
        scores = contract_last(query, keys) * SCALE + bias_ref[pl.ds(c, 1), :] + causal
        peak = jnp.max(scores, axis=1, keepdims=True)
        weights = jnp.exp2(scores - peak)
        total = jnp.sum(weights, axis=1, keepdims=True)
        mixture = jnp.dot(
            weights.astype(jnp.bfloat16), values, preferred_element_type=jnp.float32
        )
        mixture = mixture * (1.0 / total)
        level = peak + jnp.log2(total)
        high = level.astype(jnp.bfloat16).astype(jnp.float32)
        rest = level - high
        middle = rest.astype(jnp.bfloat16).astype(jnp.float32)
        stats = jnp.where(lane == 0, high, jnp.where(lane == 1, middle, rest - middle))
        both = jnp.concatenate([mixture, stats], axis=1).astype(jnp.bfloat16)
        for i, out in enumerate(outs):
            out[c] = both[i * slots : (i + 1) * slots].reshape(pairs, lines, 2 * width)

    unroll = 4

    def body(step, carry):
        for j in range(unroll):
            one(step * unroll + j)
        return carry

    lax.fori_loop(0, block // unroll, body, 0)


def attend(bias, own_k, own_v, pair_k, pair_v, queries, own):
    clusters, pairs, lines, width = own_k.shape
    block = 32
    spec = pl.BlockSpec((block, pairs, lines, width), lambda i: (i, 0, 0, 0))
    count = len(queries)
    slots = pairs * lines
    return pl.pallas_call(
        functools.partial(attend_kernel, count, own),
        grid=(clusters // block,),
        in_specs=[pl.BlockSpec((block, 2 * slots), lambda i: (i, 0))] + [spec] * (4 + count),
        out_specs=[pl.BlockSpec((block, pairs, lines, 2 * width), lambda i: (i, 0, 0, 0))]
        * count,
        out_shape=[jax.ShapeDtypeStruct((clusters, pairs, lines, 2 * width), jnp.bfloat16)]
        * count,
        compiler_params=params(),
        cost_estimate=pl.CostEstimate(
            flops=16 * clusters * slots * slots * width * count,
            bytes_accessed=30_000_000,
            transcendentals=0,
        ),
        name="attend_clusters",
    )(bias, own_k, own_v, pair_k, pair_v, *queries)


def collect_kernel(slot_ref, mixed_ref, out_ref, held):
    rows = slot_ref.shape[1]
    clusters, _, lines, width = mixed_ref.shape
    step = 256
    eye = iota((128, 128), 0) == iota((128, 128), 1)
    sub = iota((8, 128), 0)
    for side in range(2):
        wide = mixed_ref[...].reshape(clusters, lines, width).astype(jnp.float32)
        held[...] = (
            wide[:, side * RANKS : (side + 1) * RANKS]
            .reshape(clusters * RANKS, width)
            .astype(jnp.bfloat16)
        )
        levels = jnp.zeros((8, 128), jnp.float32)
        for part in range(rows // step):
            column = slot_ref[0, part * step : (part + 1) * step, side : side + 1]
            picks = as_mask(iota((step, clusters * RANKS), 1) == column)
            found = jnp.dot(picks, held[...], preferred_element_type=jnp.float32)
            out_ref[side, part * step : (part + 1) * step] = found[:, :HEAD_DIM].astype(
                jnp.bfloat16
            )
            stat = found[:, HEAD_DIM : HEAD_DIM + 1] + found[:, HEAD_DIM + 1 : HEAD_DIM + 2]
            stat = stat + found[:, HEAD_DIM + 2 : HEAD_DIM + 3]
            for piece in range(step // 128):
                line = jnp.sum(
                    jnp.where(eye, stat[piece * 128 : (piece + 1) * 128], 0.0),
                    axis=0,
                    keepdims=True,
                )
                levels = jnp.where(sub == part * (step // 128) + piece, line, levels)
        high = levels.astype(jnp.bfloat16).astype(jnp.float32)
        rest = levels - high
        middle = rest.astype(jnp.bfloat16).astype(jnp.float32)
        lines4 = jnp.concatenate(
            [high, middle, rest - middle, jnp.zeros_like(high)], axis=0
        )
        out_ref[side, rows : rows + STAT_ROWS] = lines4.astype(jnp.bfloat16)


def collect(slots, mixed, name):
    devices, rows = slots.shape
    clusters, pairs, lines, width = mixed.shape
    columns = jnp.transpose(slots.reshape(pairs, 2, rows), (0, 2, 1))
    return pl.pallas_call(
        collect_kernel,
        grid=(pairs,),
        in_specs=[
            pl.BlockSpec((1, rows, 2), lambda i: (i, 0, 0)),
            pl.BlockSpec((clusters, 1, lines, width), lambda i: (0, i, 0, 0)),
        ],
        out_specs=pl.BlockSpec((2, rows + STAT_ROWS, HEAD_DIM), lambda i: (i, 0, 0)),
        out_shape=jax.ShapeDtypeStruct((devices, rows + STAT_ROWS, HEAD_DIM), jnp.bfloat16),
        scratch_shapes=[pltpu.VMEM((clusters * RANKS, width), jnp.bfloat16)],
        compiler_params=params(),
        cost_estimate=pl.CostEstimate(
            flops=2 * devices * rows * clusters * RANKS * width,
            bytes_accessed=16_000_000,
            transcendentals=0,
        ),
        name=name,
    )(columns, mixed)


def window_kernel(first_ref, q_ref, own_k, own_v, past_k, past_v, out_ref):
    rows = q_ref.shape[0]
    step = 256
    row = iota((step, step), 0)
    column = iota((step, step), 1)

    def run(with_past):
        for part in range(rows // step):
            query = q_ref[part * step : (part + 1) * step]
            stop = (part + 1) * step
            keys, values = own_k[:stop], own_v[:stop]
            if with_past:
                keys = jnp.concatenate([past_k[part * step :], keys], axis=0)
                values = jnp.concatenate([past_v[part * step :], values], axis=0)
            scores = contract_last(query, keys)
            span = scores.shape[1]
            pieces = []
            if with_past:
                pieces.append(jnp.where(column > row, scores[:, :step], NEGATIVE))
                pieces.append(scores[:, step : span - step])
            elif span > step:
                pieces.append(scores[:, : span - step])
            pieces.append(jnp.where(column <= row, scores[:, span - step :], NEGATIVE))
            scores = jnp.concatenate(pieces, axis=1) if len(pieces) > 1 else pieces[0]
            peak = jnp.max(scores, axis=1, keepdims=True)
            weights = jnp.exp2((scores - peak) * SCALE)
            total = jnp.sum(weights, axis=1, keepdims=True)
            mixture = jnp.dot(
                weights.astype(jnp.bfloat16), values, preferred_element_type=jnp.float32
            )
            out_ref[part * step : (part + 1) * step] = (mixture * (1.0 / total)).astype(
                jnp.bfloat16
            )

    pl.when(first_ref[0] == 0)(lambda: run(False))
    pl.when(first_ref[0] != 0)(lambda: run(True))


def window_heads(my_index, query_rows, key_rows, value_rows, past):
    rows, width = query_rows.shape
    own = pl.BlockSpec((rows, HEAD_DIM), lambda h: (0, h))

    def part(index):
        return pl.BlockSpec((None, rows, HEAD_DIM), lambda h: (index, 0, h))

    return pl.pallas_call(
        window_kernel,
        grid=(HEADS_L,),
        in_specs=[pl.BlockSpec(memory_space=pltpu.SMEM), own, own, own, part(0), part(1)],
        out_specs=own,
        out_shape=jax.ShapeDtypeStruct((rows, width), jnp.bfloat16),
        compiler_params=params(),
        cost_estimate=pl.CostEstimate(
            flops=8 * HEADS_L * rows * 1280 * HEAD_DIM,
            bytes_accessed=14_000_000,
            transcendentals=0,
        ),
        name="window_heads",
    )(my_index.reshape(1), query_rows, key_rows, value_rows, past, past)


def merge_kernel(count, valid_ref, base_ref, *refs):
    del base_ref
    parts, out_ref = refs[:count], refs[count]
    rows = out_ref.shape[0]
    eye = iota((128, 128), 0) == iota((128, 128), 1)
    levels = []
    for i, part in enumerate(parts):
        stats = part[rows : rows + STAT_ROWS].astype(jnp.float32)
        level = stats[0:8] + stats[8:16] + stats[16:24]
        levels.append(jnp.where(valid_ref[i] != 0, level, NEGATIVE))
    peak = functools.reduce(jnp.maximum, levels)
    shares = [jnp.exp2(level - peak) for level in levels]
    whole = functools.reduce(jnp.add, shares)
    shares = [share / whole for share in shares]
    for piece in range(rows // 128):
        here = slice(piece * 128, (piece + 1) * 128)
        result = jnp.zeros((128, HEAD_DIM), jnp.float32)
        for part, share in zip(parts, shares):
            column = jnp.sum(
                jnp.where(eye, share[piece : piece + 1], 0.0), axis=1, keepdims=True
            )
            result = result + part[here].astype(jnp.float32) * column
        out_ref[here] = result.astype(jnp.bfloat16)


def merge(base, parts, valid):
    rows, width = base.shape
    spec = pl.BlockSpec((None, rows + STAT_ROWS, HEAD_DIM), lambda h: (h, 0, 0))
    return pl.pallas_call(
        functools.partial(merge_kernel, len(parts)),
        grid=(HEADS_R,),
        in_specs=[pl.BlockSpec(memory_space=pltpu.SMEM), pl.BlockSpec(memory_space=pl.ANY)]
        + [spec] * len(parts),
        out_specs=pl.BlockSpec((rows, HEAD_DIM), lambda h: (0, HEADS_L + h)),
        out_shape=jax.ShapeDtypeStruct((rows, width), jnp.bfloat16),
        input_output_aliases={1: 0},
        compiler_params=params(),
        name="merge_parts",
    )(valid, base, *parts)


def on_device(query_rows, key_rows, value_rows, cluster_ids):
    rows = query_rows.shape[0]
    local_width = HEADS_L * HEAD_DIM
    device_count = lax.axis_size(AXES)
    my_index = lax.axis_index(AXES)
    group = HEADS_R
    planes = device_count // group
    couples = planes // 2
    plane = my_index // group
    groups = [[group * i + j for j in range(group)] for i in range(planes)]

    def swap(array):
        return lax.all_to_all(
            array, AXES, split_axis=0, concat_axis=0, tiled=True, axis_index_groups=groups
        )

    def move(array, routes):
        pairs = [(group * a + j, group * b + j) for a, b in routes for j in range(group)]
        return lax.ppermute(array, AXES, pairs)

    def heads_first(matrix):
        routed = matrix[:, local_width:].reshape(rows, HEADS_R, HEAD_DIM)
        return jnp.transpose(routed, (1, 0, 2))

    swapped = swap(
        jnp.stack([heads_first(m) for m in (query_rows, key_rows, value_rows)], axis=1)
    )
    slots, counts = rank_tokens(cluster_ids)
    facts = lax.all_gather(jnp.concatenate([slots, counts], axis=1), AXES)
    facts = lax.dynamic_index_in_dim(facts, my_index % group, 1, keepdims=False)
    facts = facts.reshape(planes, group, rows + CLUSTERS)

    def slots_of(index):
        return lax.dynamic_index_in_dim(facts, index, 0, keepdims=False)[:, :rows]

    def bias_of(index):
        held = lax.dynamic_index_in_dim(facts, index, 0, keepdims=False)[:, rows:]
        filled = jnp.arange(RANKS, dtype=jnp.int32)[None, None, :] < held.T[:, :, None]
        return jnp.where(filled, 0.0, NEGATIVE).reshape(CLUSTERS, group * RANKS)

    partner = plane ^ 1
    is_odd = plane % 2 == 1
    pair_rows = move(swapped[:, 1:], [(2 * j, 2 * j + 1) for j in range(couples)])
    queries = swapped[:, 0]

    def visit(queries, shift):
        found = []
        for side in range(2):
            routes = [(2 * j + side, 2 * (j - shift) + 1) for j in range(shift, couples)]
            found.append(move(queries, routes))
        return found

    visitors = visit(queries, 1) if couples > 1 else []
    past = lax.ppermute(
        jnp.stack([key_rows[:, :local_width], value_rows[:, :local_width]]),
        AXES,
        [(i, i + 1) for i in range(device_count - 1)],
    )

    own_q, own_k, own_v = dispatch(
        slots_of(plane), [(swapped, 0), (swapped, 1), (swapped, 2)], "dispatch_own"
    )
    pair_k, pair_v = dispatch(slots_of(partner), [(pair_rows, 0), (pair_rows, 1)], "dispatch_pair")
    bias = jnp.concatenate(
        [bias_of(plane), jnp.where(is_odd, bias_of(partner), NEGATIVE)], axis=1
    )

    def visit_slots(shift):
        homes = [2 * (plane // 2 + shift) + side for side in range(2)]
        return [slots_of(jnp.minimum(home, planes - 1)) for home in homes]

    def give_back(mixed, slots, shift):
        back = []
        for side in range(2):
            found = collect(slots[side], mixed[side], "collect_visit")
            routes = [(2 * (j - shift) + 1, 2 * j + side) for j in range(shift, couples)]
            back.append(move(found, routes))
        return swap(jnp.where(is_odd, back[1], back[0]))

    kept = (bias, own_k, own_v, pair_k, pair_v)
    asked = [own_q]
    homes = visit_slots(1)
    for side, moved in enumerate(visitors):
        asked += dispatch(homes[side], [(moved, None)], "dispatch_visit")
    mixed = attend(*kept, asked, True)
    parts = [swap(collect(slots_of(plane), mixed[0], "collect_own"))]
    if couples > 1:
        parts.append(give_back(mixed[1:], homes, 1))
    for shift in range(2, couples):
        queries, parts[-1] = lax.optimization_barrier((queries, parts[-1]))
        homes = visit_slots(shift)
        asked = []
        for side, moved in enumerate(visit(queries, shift)):
            asked += dispatch(homes[side], [(moved, None)], "dispatch_visit")
        parts.append(give_back(attend(*kept, asked, False), homes, shift))
    valid = [jnp.int32(1)] + [(plane // 2 >= s).astype(jnp.int32) for s in range(1, couples)]
    local_out = window_heads(my_index, query_rows, key_rows, value_rows, past)
    return merge(local_out, parts, jnp.stack(valid))


def solution(mesh):
    return jax.shard_map(
        on_device,
        mesh=mesh,
        in_specs=(P(AXES, None), P(AXES, None), P(AXES, None), P(None, AXES)),
        out_specs=P(AXES, None),
        check_vma=False,
    )
```

```python
import functools

import jax
import jax.numpy as jnp
from jax import lax
from jax.experimental import pallas as pl
from jax.experimental.pallas import tpu as pltpu
from jax.sharding import PartitionSpec as P

HEADS_L = 8
HEADS_R = 8
HEAD_DIM = 128
WINDOW = 1024
CLUSTERS = 256

RANKS = 8
NEGATIVE = -(2.0**100)
AXES = ("seq", "grp")
SCALE = HEAD_DIM ** (-0.5) * 1.4426950408889634
STAT_ROWS = 16
HALVES = 2
VMEM = 56 * 1024 * 1024


def params(**extra):
    return pltpu.CompilerParams(vmem_limit_bytes=VMEM, **extra)


def contract_last(a, b):
    return lax.dot_general(a, b, (((1,), (1,)), ((), ())), preferred_element_type=jnp.float32)


def iota(shape, dim):
    return lax.broadcasted_iota(jnp.int32, shape, dim)


def as_mask(condition):
    return jnp.where(condition, 1.0, 0.0).astype(jnp.bfloat16)


def rank_kernel(ids_ref, slot_ref, count_ref):
    heads, rows = ids_ref.shape
    before = as_mask(iota((rows, rows), 0) < iota((rows, rows), 1))
    ones = jnp.ones((8, rows), jnp.bfloat16)
    for head in range(heads):
        ids = ids_ref[head : head + 1, :]
        members = as_mask(iota((CLUSTERS, rows), 0) == ids)
        earlier = jnp.dot(members, before, preferred_element_type=jnp.float32)
        rank = jnp.sum(members.astype(jnp.float32) * earlier, axis=0, keepdims=True)
        slot_ref[head : head + 1, :] = ids * RANKS + rank.astype(jnp.int32)
        count_ref[head : head + 1, :] = contract_last(ones, members)[0:1].astype(jnp.int32)


def rank_tokens(cluster_ids):
    heads, rows = cluster_ids.shape
    return pl.pallas_call(
        rank_kernel,
        out_shape=(
            jax.ShapeDtypeStruct((heads, rows), jnp.int32),
            jax.ShapeDtypeStruct((heads, CLUSTERS), jnp.int32),
        ),
        compiler_params=params(),
        name="rank_tokens",
    )(cluster_ids)


def near(ids, base, step):
    here = ids - base
    return jnp.where((here >= 0) & (here < step), here, -1).astype(jnp.float32).astype(jnp.bfloat16)


def equal_mask(a, b):
    one, zero = jnp.bfloat16(1.0), jnp.bfloat16(0.0)
    return jnp.where(a == b, one, zero)


def dispatch_rows(slot_ref, read, outs):
    rows = slot_ref.shape[-1]
    fine = 256
    step = 1024
    lines = iota((fine, rows), 0).astype(jnp.float32).astype(jnp.bfloat16)

    def body(part, carry):
        base = part * step
        halves = []
        for side in range(2):
            ids = slot_ref[0, side : side + 1, :]
            picks = jnp.concatenate(
                [
                    equal_mask(
                        lines, jnp.broadcast_to(near(ids, base + i, fine), (fine, rows))
                    )
                    for i in range(0, step, fine)
                ],
                axis=0,
            )
            found = jnp.dot(picks, read(side), preferred_element_type=jnp.float32)
            halves.append(found.reshape(step // RANKS, RANKS, len(outs) * HEAD_DIM))
        joined = jnp.concatenate(halves, axis=1).astype(jnp.bfloat16)
        for i, out in enumerate(outs):
            out[pl.ds(part * (step // RANKS), step // RANKS), 0] = joined[
                :, :, i * HEAD_DIM : (i + 1) * HEAD_DIM
            ]
        return carry

    lax.fori_loop(0, CLUSTERS * RANKS // step, body, 0)


def dispatch_kernel(count, slot_ref, *refs):
    sources, outs = refs[:count], refs[count:]
    rows = slot_ref.shape[-1]

    def read(side):
        return jnp.concatenate([s[side].reshape(rows, HEAD_DIM) for s in sources], axis=1)

    dispatch_rows(slot_ref, read, outs)


def slot_block(index):
    return pl.BlockSpec((CLUSTERS, 1, 2 * RANKS, HEAD_DIM), index)


def dispatch(slots, arrays, name):
    devices, rows = slots.shape
    pairs = devices // 2
    in_specs = [pl.BlockSpec((1, 2, rows), lambda i: (i, 0, 0))]
    operands = [slots.reshape(pairs, 2, rows)]
    for array, part in arrays:
        if part is None:
            in_specs.append(pl.BlockSpec((2, rows, HEAD_DIM), lambda i: (i, 0, 0)))
        else:
            in_specs.append(
                pl.BlockSpec((2, 1, rows, HEAD_DIM), lambda i, part=part: (i, part, 0, 0))
            )
        operands.append(array)
    count = len(arrays)
    shape = (CLUSTERS, pairs, 2 * RANKS, HEAD_DIM)
    flops = 2 * devices * rows * CLUSTERS * RANKS * HEAD_DIM * count
    return pl.pallas_call(
        functools.partial(dispatch_kernel, count),
        grid=(pairs,),
        in_specs=in_specs,
        out_specs=[slot_block(lambda i: (0, i, 0, 0))] * count,
        out_shape=[jax.ShapeDtypeStruct(shape, jnp.bfloat16)] * count,
        compiler_params=params(),
        cost_estimate=pl.CostEstimate(
            flops=flops, bytes_accessed=12_000_000 * count, transcendentals=0
        ),
        name=name,
    )(*operands)


def attend_clusters(own, bias_ref, own_k, own_v, pair_k, pair_v, query, mixed, start):
    block, pairs, lines, width = own_k.shape
    slots = pairs * lines
    batch = 32
    lane = iota((slots, 2 * slots), 1)
    row = iota((slots, 2 * slots), 0)
    causal = jnp.where((lane <= row) | (lane >= slots), 0.0, NEGATIVE)
    lane = iota((1, 128), 1)
    ones = jnp.ones((4 * slots, 128), jnp.bfloat16)
    none = jnp.zeros((slots, 2 * slots), jnp.bfloat16)

    def read(ref, c):
        return ref[c].reshape(slots, width)

    def body(step, carry):
        base = step * batch
        pieces = []
        for j in range(0, batch, 2):
            here = (base + j, base + j + 1)
            keys = [read(ref, c) for c in here for ref in (own_k, pair_k)]
            asked = [read(query, c) for c in here]
            scores = contract_last(jnp.concatenate(asked, axis=0), jnp.concatenate(keys, axis=0))
            for i, c in enumerate(here):
                part = scores[i * slots : (i + 1) * slots, i * 2 * slots : (i + 1) * 2 * slots]
                part = part + bias_ref[pl.ds(c, 1), :]
                pieces.append(part + causal if own else part)
        scores = jnp.concatenate(pieces, axis=0)
        peak = jnp.max(scores, axis=1, keepdims=True)
        upper = peak.astype(jnp.bfloat16).astype(jnp.float32)
        lower = (peak - upper).astype(jnp.bfloat16).astype(jnp.float32)
        peak = upper + lower
        weights = jnp.exp2((scores - peak) * SCALE)
        weights = weights.astype(jnp.bfloat16)
        pieces = []
        for j in range(0, batch, 2):
            here = (base + j, base + j + 1)
            values = [read(ref, c) for c in here for ref in (own_v, pair_v)]
            values = jnp.concatenate([jnp.concatenate(values, axis=0), ones], axis=1)
            first = jnp.concatenate([weights[j * slots : (j + 1) * slots], none], axis=1)
            second = jnp.concatenate([none, weights[(j + 1) * slots : (j + 2) * slots]], axis=1)
            pieces.append(
                jnp.dot(
                    jnp.concatenate([first, second], axis=0),
                    values,
                    preferred_element_type=jnp.float32,
                )
            )
        mixture = jnp.concatenate(pieces, axis=0)
        total = mixture[:, width:]
        mixture = mixture[:, :width] * (1.0 / total)
        high = total.astype(jnp.bfloat16).astype(jnp.float32)
        stats = jnp.where(lane == 2, high, total - high)
        stats = jnp.where(lane == 0, upper, jnp.where(lane == 1, lower, stats))
        both = jnp.concatenate([mixture, stats], axis=1).astype(jnp.bfloat16)
        mixed[pl.ds(start + base, batch)] = both.reshape(batch, pairs, lines, 2 * width)
        return carry

    lax.fori_loop(0, block // batch, body, 0)


def collect_rows(index, slot_ref, mixed, outs, held):
    rows = slot_ref.shape[1]
    clusters, _, lines, width = mixed.shape
    step = 256
    eye = iota((128, 128), 0) == iota((128, 128), 1)
    part_rows = rows // HALVES
    chunks = part_rows // 128
    sub = iota((chunks, 128), 0)

    def as_line(column):
        return jnp.sum(jnp.where(eye, column, 0.0), axis=0, keepdims=True)

    for side in range(2):
        wide = mixed[:, pl.ds(index, 1)].reshape(clusters, lines, width).astype(jnp.float32)
        held[...] = (
            wide[:, side * RANKS : (side + 1) * RANKS]
            .reshape(clusters * RANKS, width)
            .astype(jnp.bfloat16)
        )
        for half, out_ref in enumerate(outs):
            peaks = jnp.zeros((chunks, 128), jnp.float32)
            totals = jnp.zeros((chunks, 128), jnp.float32)
            for first in range(0, part_rows, step):
                start = half * part_rows + first
                column = slot_ref[0, start : start + step, side : side + 1]
                picks = as_mask(iota((step, clusters * RANKS), 1) == column)
                found = jnp.dot(picks, held[...], preferred_element_type=jnp.float32)
                out_ref[side, first : first + step] = found[:, :HEAD_DIM].astype(jnp.bfloat16)
                stat = [found[:, HEAD_DIM + i : HEAD_DIM + i + 1] for i in range(4)]
                peak, total = stat[0] + stat[1], stat[2] + stat[3]
                for piece in range(step // 128):
                    here = slice(piece * 128, (piece + 1) * 128)
                    place = sub == first // 128 + piece
                    peaks = jnp.where(place, as_line(peak[here]), peaks)
                    totals = jnp.where(place, as_line(total[here]), totals)
            upper = peaks.astype(jnp.bfloat16).astype(jnp.float32)
            high = totals.astype(jnp.bfloat16).astype(jnp.float32)
            stats = jnp.concatenate([upper, peaks - upper, high, totals - high], axis=0)
            out_ref[side, part_rows : part_rows + STAT_ROWS] = stats.astype(jnp.bfloat16)


def answer_kernel(own, steps, bias_ref, own_k, own_v, pair_k, pair_v, query, slot_ref, *refs):
    *outs, mixed, held = refs
    step = pl.program_id(0)
    block = own_k.shape[0]

    @pl.when(step < steps)
    def _():
        attend_clusters(
            own, bias_ref, own_k, own_v, pair_k, pair_v, query, mixed, step * block
        )

    @pl.when(step >= steps)
    def _():
        collect_rows(step - steps, slot_ref, mixed, outs, held)


def answer(bias, own_k, own_v, pair_k, pair_v, query, slots, own, name):
    clusters, pairs, lines, width = own_k.shape
    devices, rows = slots.shape
    block = 64
    steps = clusters // block
    columns = jnp.transpose(slots.reshape(pairs, 2, rows), (0, 2, 1))
    tall = rows // HALVES + STAT_ROWS
    last = steps - 1
    spec = pl.BlockSpec(
        (block, pairs, lines, width), lambda i: (jnp.minimum(i, last), 0, 0, 0)
    )
    return pl.pallas_call(
        functools.partial(answer_kernel, own, steps),
        grid=(steps + pairs,),
        in_specs=[pl.BlockSpec((block, 2 * pairs * lines), lambda i: (jnp.minimum(i, last), 0))]
        + [spec] * 5
        + [pl.BlockSpec((1, rows, 2), lambda i: (jnp.maximum(i - steps, 0), 0, 0))],
        out_specs=[
            pl.BlockSpec((2, tall, HEAD_DIM), lambda i: (jnp.maximum(i - steps, 0), 0, 0))
        ]
        * HALVES,
        out_shape=[jax.ShapeDtypeStruct((devices, tall, HEAD_DIM), jnp.bfloat16)] * HALVES,
        scratch_shapes=[
            pltpu.VMEM((clusters, pairs, lines, 2 * width), jnp.bfloat16),
            pltpu.VMEM((clusters * RANKS, 2 * width), jnp.bfloat16),
        ],
        compiler_params=params(),
        cost_estimate=pl.CostEstimate(
            flops=2 * devices * rows * clusters * RANKS * 2 * width,
            bytes_accessed=30_000_000,
            transcendentals=0,
        ),
        name=name,
    )(bias, own_k, own_v, pair_k, pair_v, query, columns)


def window_kernel(first_ref, q_ref, own_k, own_v, past_k, past_v, out_ref):
    rows = q_ref.shape[0]
    step = 256
    row = iota((step, step), 0)
    column = iota((step, step), 1)

    def run(with_past):
        for part in range(rows // step):
            query = q_ref[part * step : (part + 1) * step]
            stop = (part + 1) * step
            keys, values = own_k[:stop], own_v[:stop]
            if with_past:
                keys = jnp.concatenate([past_k[part * step :], keys], axis=0)
                values = jnp.concatenate([past_v[part * step :], values], axis=0)
            scores = contract_last(query, keys)
            span = scores.shape[1]
            pieces = []
            if with_past:
                pieces.append(jnp.where(column > row, scores[:, :step], NEGATIVE))
                pieces.append(scores[:, step : span - step])
            elif span > step:
                pieces.append(scores[:, : span - step])
            pieces.append(jnp.where(column <= row, scores[:, span - step :], NEGATIVE))
            scores = jnp.concatenate(pieces, axis=1) if len(pieces) > 1 else pieces[0]
            peak = jnp.max(scores, axis=1, keepdims=True)
            weights = jnp.exp2((scores - peak) * SCALE)
            total = jnp.sum(weights, axis=1, keepdims=True)
            mixture = jnp.dot(
                weights.astype(jnp.bfloat16), values, preferred_element_type=jnp.float32
            )
            out_ref[part * step : (part + 1) * step] = (mixture * (1.0 / total)).astype(
                jnp.bfloat16
            )

    pl.when(first_ref[0] == 0)(lambda: run(False))
    pl.when(first_ref[0] != 0)(lambda: run(True))


def window_heads(my_index, query_rows, key_rows, value_rows, past):
    rows, width = query_rows.shape
    own = pl.BlockSpec((rows, HEAD_DIM), lambda h: (0, h))
    return pl.pallas_call(
        window_kernel,
        grid=(HEADS_L,),
        in_specs=[pl.BlockSpec(memory_space=pltpu.SMEM)] + [own] * 5,
        out_specs=own,
        out_shape=jax.ShapeDtypeStruct((rows, width), jnp.bfloat16),
        compiler_params=params(),
        cost_estimate=pl.CostEstimate(
            flops=8 * HEADS_L * rows * 1280 * HEAD_DIM,
            bytes_accessed=14_000_000,
            transcendentals=0,
        ),
        name="window_heads",
    )(my_index.reshape(1), query_rows, key_rows, value_rows, *past)


def merge_kernel(count, valid_ref, *refs):
    parts, out_ref = refs[:count], refs[count]
    rows = out_ref.shape[0]
    eye = iota((128, 128), 0) == iota((128, 128), 1)
    n = rows // 128
    peaks, totals = [], []
    for i, part in enumerate(parts):
        stats = part[rows : rows + STAT_ROWS].astype(jnp.float32)
        peaks.append(jnp.where(valid_ref[i] != 0, stats[:n] + stats[n : 2 * n], NEGATIVE))
        totals.append(stats[2 * n : 3 * n] + stats[3 * n : 4 * n])
    highest = functools.reduce(jnp.maximum, peaks)
    shares = [t * jnp.exp2((peak - highest) * SCALE) for t, peak in zip(totals, peaks)]
    whole = functools.reduce(jnp.add, shares)
    shares = [share / whole for share in shares]
    for piece in range(n):
        here = slice(piece * 128, (piece + 1) * 128)
        result = jnp.zeros((128, HEAD_DIM), jnp.float32)
        for part, share in zip(parts, shares):
            column = jnp.sum(
                jnp.where(eye, share[piece : piece + 1], 0.0), axis=1, keepdims=True
            )
            result = result + part[here].astype(jnp.float32) * column
        out_ref[here] = result.astype(jnp.bfloat16)


def merge(parts, valid):
    devices, tall, width = parts[0].shape
    rows = tall - STAT_ROWS
    return pl.pallas_call(
        functools.partial(merge_kernel, len(parts)),
        grid=(devices,),
        in_specs=[pl.BlockSpec(memory_space=pltpu.SMEM)]
        + [pl.BlockSpec((None, tall, width), lambda i: (i, 0, 0))] * len(parts),
        out_specs=pl.BlockSpec((None, rows, width), lambda i: (i, 0, 0)),
        out_shape=jax.ShapeDtypeStruct((devices, rows, width), jnp.bfloat16),
        compiler_params=params(),
        name="merge_parts",
    )(valid, *parts)


def place_kernel(base_ref, heads_ref, out_ref):
    del base_ref
    for head in range(HEADS_R):
        out_ref[:, head * HEAD_DIM : (head + 1) * HEAD_DIM] = heads_ref[head]


def place_heads(base, heads, half):
    rows, width = base.shape
    block = 256
    steps = rows // HALVES // block
    return pl.pallas_call(
        place_kernel,
        grid=(steps,),
        in_specs=[
            pl.BlockSpec(memory_space=pl.ANY),
            pl.BlockSpec((HEADS_R, block, HEAD_DIM), lambda i: (0, i, 0)),
        ],
        out_specs=pl.BlockSpec((block, HEADS_R * HEAD_DIM), lambda i: (half * steps + i, 1)),
        out_shape=jax.ShapeDtypeStruct((rows, width), jnp.bfloat16),
        input_output_aliases={0: 0},
        compiler_params=params(),
        name="place_heads",
    )(base, heads)


def heads_kernel(in_ref, out_ref):
    for head in range(HEADS_R):
        out_ref[head] = in_ref[:, head * HEAD_DIM : (head + 1) * HEAD_DIM]


def heads_first(matrix):
    rows = matrix.shape[0]
    block = 256
    return pl.pallas_call(
        heads_kernel,
        grid=(rows // block,),
        in_specs=[pl.BlockSpec((block, HEADS_R * HEAD_DIM), lambda i: (i, 1))],
        out_specs=pl.BlockSpec((HEADS_R, block, HEAD_DIM), lambda i: (0, i, 0)),
        out_shape=jax.ShapeDtypeStruct((HEADS_R, rows, HEAD_DIM), jnp.bfloat16),
        compiler_params=params(),
        name="heads_first",
    )(matrix)


def on_device(query_rows, key_rows, value_rows, cluster_ids):
    rows = query_rows.shape[0]
    local_width = HEADS_L * HEAD_DIM
    device_count = lax.axis_size(AXES)
    my_index = lax.axis_index(AXES)
    group = HEADS_R
    planes = device_count // group
    couples = planes // 2
    plane = my_index // group
    place = my_index % group
    groups = [[group * i + j for j in range(group)] for i in range(planes)]

    def swap(array):
        return lax.all_to_all(
            array, AXES, split_axis=0, concat_axis=0, tiled=True, axis_index_groups=groups
        )

    def move(array, routes):
        pairs = [(group * a + j, group * b + j) for a, b in routes for j in range(group)]
        return lax.ppermute(array, AXES, pairs)

    def after(array, *others):
        return lax.optimization_barrier((array, *others))

    slots, counts = rank_tokens(cluster_ids)
    facts = lax.all_gather(jnp.concatenate([slots, counts], axis=1), AXES)
    facts = lax.dynamic_index_in_dim(facts, place, 1, keepdims=False)
    facts = facts.reshape(planes, group, rows + CLUSTERS)

    def visit_routes(shift, side):
        return [(2 * j + side, 2 * (j - shift) + 1) for j in range(shift, couples)]

    pair_routes = [(2 * j, 2 * j + 1) for j in range(couples)]
    keys = swap(heads_first(key_rows))
    pair_keys = move(keys, pair_routes)
    q_heads, keys = after(heads_first(query_rows), keys)
    queries = swap(q_heads)

    def visit(queries, shift):
        first = move(queries, visit_routes(shift, 0))
        queries, first = after(queries, first)
        return [first, move(queries, visit_routes(shift, 1))]

    visitors = visit(queries, 1) if couples > 1 else []
    v_heads, queries = after(heads_first(value_rows), queries)
    values = swap(v_heads)
    pair_values = move(values, pair_routes)
    past = [key_rows[:, :local_width], value_rows[:, :local_width]]
    *past, pair_values = after(past[0], past[1], pair_values)
    past = [lax.ppermute(m, AXES, [(i, i + 1) for i in range(device_count - 1)]) for m in past]

    def facts_of(index):
        return lax.dynamic_index_in_dim(facts, index, 0, keepdims=False)

    def bias_of(held):
        filled = jnp.arange(RANKS, dtype=jnp.int32)[None, None, :] < held.T[:, :, None]
        return jnp.where(filled, 0.0, NEGATIVE).reshape(CLUSTERS, group * RANKS)

    def visit_slots(shift):
        homes = [2 * (plane // 2 + shift) + side for side in range(2)]
        return [facts_of(jnp.minimum(home, planes - 1))[:, :rows] for home in homes]

    own_facts = facts_of(plane)
    pair_facts = facts_of(plane ^ 1)
    is_odd = plane % 2 == 1
    bias = jnp.concatenate(
        [bias_of(own_facts[:, rows:]), jnp.where(is_odd, bias_of(pair_facts[:, rows:]), NEGATIVE)],
        axis=1,
    )
    own_q, own_k, own_v = dispatch(
        own_facts[:, :rows], [(queries, None), (keys, None), (values, None)], "dispatch_own"
    )
    (pair_k,) = dispatch(pair_facts[:, :rows], [(pair_keys, None)], "dispatch_pair_keys")
    homes = visit_slots(1)
    asked = []
    if couples > 1:
        asked = list(dispatch(homes[0], [(visitors[0], None)], "dispatch_visit"))
        pair_values, pair_k, own_q, asked[0] = after(pair_values, pair_k, own_q, asked[0])
    (pair_v,) = dispatch(pair_facts[:, :rows], [(pair_values, None)], "dispatch_pair_values")
    kept = (bias, own_k, own_v, pair_k, pair_v)

    parts, valid = [], [jnp.int32(1)]
    for shift in range(1, couples):
        homes = visit_slots(shift)
        if shift > 1:
            queries, parts[-1][-1] = after(queries, parts[-1][-1])
            visitors = visit(queries, shift)
            asked = list(dispatch(homes[0], [(visitors[0], None)], "dispatch_visit"))
        for side in range(2):
            if side == 1:
                asked = dispatch(homes[1], [(visitors[1], None)], "dispatch_visit")
            found = list(answer(*kept, asked[0], homes[side], False, "answer_visit"))
            if side == 0:
                visitors[1], found[0] = after(visitors[1], found[0])
            elif shift == 1:
                own_q, found[0] = after(own_q, found[0])
            routes = [(b, a) for a, b in visit_routes(shift, side)]
            back = []
            for half in range(HALVES):
                if half:
                    found[half], back[-1] = after(found[half], back[-1])
                back.append(move(found[half], routes))
            parts.append(back)
            valid.append(((plane // 2 >= shift) & (plane % 2 == side)).astype(jnp.int32))
    own_found = list(answer(*kept, own_q, own_facts[:, :rows], True, "answer_own"))
    past[0], own_found[0] = after(past[0], own_found[0])
    result = window_heads(my_index, query_rows, key_rows, value_rows, past)
    valid = jnp.stack(valid)
    if parts:
        parts[-1][0], result = after(parts[-1][0], result)
    merged = []
    for half in range(HALVES):
        joined = merge([own_found[half]] + [back[half] for back in parts], valid)
        if half:
            joined, merged[-1] = after(joined, merged[-1])
        merged.append(swap(joined))
    for half in range(HALVES):
        result = place_heads(result, merged[half], half)
    return result


def solution(mesh):
    return jax.shard_map(
        on_device,
        mesh=mesh,
        in_specs=(P(AXES, None), P(AXES, None), P(AXES, None), P(None, AXES)),
        out_specs=P(AXES, None),
        check_vma=False,
    )
```

```python
import functools

import jax
import jax.numpy as jnp
from jax import lax
from jax.experimental import pallas as pl
from jax.experimental.pallas import tpu as pltpu
from jax.sharding import PartitionSpec as P

HEADS_L = 8
HEADS_R = 8
HEAD_DIM = 128
WINDOW = 1024
CLUSTERS = 256

RANKS = 8
NEGATIVE = -(2.0**100)
AXES = ("seq", "grp")
SCALE = HEAD_DIM ** (-0.5) * 1.4426950408889634
STAT_ROWS = 16
HALVES = 2
VMEM = 56 * 1024 * 1024


def params(**extra):
    return pltpu.CompilerParams(vmem_limit_bytes=VMEM, **extra)


def contract_last(a, b):
    return lax.dot_general(a, b, (((1,), (1,)), ((), ())), preferred_element_type=jnp.float32)


def iota(shape, dim):
    return lax.broadcasted_iota(jnp.int32, shape, dim)


def as_mask(condition):
    return jnp.where(condition, 1.0, 0.0).astype(jnp.bfloat16)


def rank_kernel(ids_ref, slot_ref, count_ref):
    heads, rows = ids_ref.shape
    before = as_mask(iota((rows, rows), 0) < iota((rows, rows), 1))
    ones = jnp.ones((8, rows), jnp.bfloat16)
    for head in range(heads):
        ids = ids_ref[head : head + 1, :]
        members = as_mask(iota((CLUSTERS, rows), 0) == ids)
        earlier = jnp.dot(members, before, preferred_element_type=jnp.float32)
        rank = jnp.sum(members.astype(jnp.float32) * earlier, axis=0, keepdims=True)
        slot_ref[head : head + 1, :] = ids * RANKS + rank.astype(jnp.int32)
        count_ref[head : head + 1, :] = contract_last(ones, members)[0:1].astype(jnp.int32)


def rank_tokens(cluster_ids):
    heads, rows = cluster_ids.shape
    return pl.pallas_call(
        rank_kernel,
        out_shape=(
            jax.ShapeDtypeStruct((heads, rows), jnp.int32),
            jax.ShapeDtypeStruct((heads, CLUSTERS), jnp.int32),
        ),
        compiler_params=params(),
        name="rank_tokens",
    )(cluster_ids)


def near(ids, base, step):
    here = ids - base
    return jnp.where((here >= 0) & (here < step), here, -1).astype(jnp.float32).astype(jnp.bfloat16)


def equal_mask(a, b):
    one, zero = jnp.bfloat16(1.0), jnp.bfloat16(0.0)
    return jnp.where(a == b, one, zero)


def dispatch_rows(slot_ref, read, outs):
    rows = slot_ref.shape[-1]
    fine = 256
    step = 1024
    lines = iota((fine, rows), 0).astype(jnp.float32).astype(jnp.bfloat16)

    def body(part, carry):
        base = part * step
        halves = []
        for side in range(2):
            ids = slot_ref[0, side : side + 1, :]
            picks = jnp.concatenate(
                [
                    equal_mask(
                        lines, jnp.broadcast_to(near(ids, base + i, fine), (fine, rows))
                    )
                    for i in range(0, step, fine)
                ],
                axis=0,
            )
            found = jnp.dot(picks, read(side), preferred_element_type=jnp.float32)
            halves.append(found.reshape(step // RANKS, RANKS, len(outs) * HEAD_DIM))
        joined = jnp.concatenate(halves, axis=1).astype(jnp.bfloat16)
        for i, out in enumerate(outs):
            out[pl.ds(part * (step // RANKS), step // RANKS), 0] = joined[
                :, :, i * HEAD_DIM : (i + 1) * HEAD_DIM
            ]
        return carry

    lax.fori_loop(0, CLUSTERS * RANKS // step, body, 0)


def dispatch_kernel(count, slot_ref, *refs):
    sources, outs = refs[:count], refs[count:]
    rows = slot_ref.shape[-1]

    def read(side):
        return jnp.concatenate([s[side].reshape(rows, HEAD_DIM) for s in sources], axis=1)

    dispatch_rows(slot_ref, read, outs)


def slot_block(index):
    return pl.BlockSpec((CLUSTERS, 1, 2 * RANKS, HEAD_DIM), index)


def dispatch(slots, arrays, name):
    devices, rows = slots.shape
    pairs = devices // 2
    in_specs = [pl.BlockSpec((1, 2, rows), lambda i: (i, 0, 0))]
    operands = [slots.reshape(pairs, 2, rows)]
    for array, part in arrays:
        if part is None:
            in_specs.append(pl.BlockSpec((2, rows, HEAD_DIM), lambda i: (i, 0, 0)))
        else:
            in_specs.append(
                pl.BlockSpec((2, 1, rows, HEAD_DIM), lambda i, part=part: (i, part, 0, 0))
            )
        operands.append(array)
    count = len(arrays)
    shape = (CLUSTERS, pairs, 2 * RANKS, HEAD_DIM)
    flops = 2 * devices * rows * CLUSTERS * RANKS * HEAD_DIM * count
    return pl.pallas_call(
        functools.partial(dispatch_kernel, count),
        grid=(pairs,),
        in_specs=in_specs,
        out_specs=[slot_block(lambda i: (0, i, 0, 0))] * count,
        out_shape=[jax.ShapeDtypeStruct(shape, jnp.bfloat16)] * count,
        compiler_params=params(),
        cost_estimate=pl.CostEstimate(
            flops=flops, bytes_accessed=12_000_000 * count, transcendentals=0
        ),
        name=name,
    )(*operands)


def attend_clusters(own, bias_ref, own_k, own_v, pair_k, pair_v, query, mixed, start):
    block, pairs, lines, width = own_k.shape
    slots = pairs * lines
    batch = 32
    lane = iota((slots, 2 * slots), 1)
    row = iota((slots, 2 * slots), 0)
    causal = jnp.where((lane <= row) | (lane >= slots), 0.0, NEGATIVE)
    lane = iota((1, 128), 1)
    ones = jnp.ones((4 * slots, 128), jnp.bfloat16)
    none = jnp.zeros((slots, 2 * slots), jnp.bfloat16)

    def read(ref, c):
        return ref[c].reshape(slots, width)

    def body(step, carry):
        base = step * batch
        pieces = []
        for j in range(0, batch, 2):
            here = (base + j, base + j + 1)
            keys = [read(ref, c) for c in here for ref in (own_k, pair_k)]
            asked = [read(query, c) for c in here]
            scores = contract_last(jnp.concatenate(asked, axis=0), jnp.concatenate(keys, axis=0))
            for i, c in enumerate(here):
                part = scores[i * slots : (i + 1) * slots, i * 2 * slots : (i + 1) * 2 * slots]
                part = part + bias_ref[pl.ds(c, 1), :]
                pieces.append(part + causal if own else part)
        scores = jnp.concatenate(pieces, axis=0)
        peak = jnp.max(scores, axis=1, keepdims=True)
        upper = peak.astype(jnp.bfloat16).astype(jnp.float32)
        lower = (peak - upper).astype(jnp.bfloat16).astype(jnp.float32)
        peak = upper + lower
        weights = jnp.exp2((scores - peak) * SCALE)
        weights = weights.astype(jnp.bfloat16)
        pieces = []
        for j in range(0, batch, 2):
            here = (base + j, base + j + 1)
            values = [read(ref, c) for c in here for ref in (own_v, pair_v)]
            values = jnp.concatenate([jnp.concatenate(values, axis=0), ones], axis=1)
            first = jnp.concatenate([weights[j * slots : (j + 1) * slots], none], axis=1)
            second = jnp.concatenate([none, weights[(j + 1) * slots : (j + 2) * slots]], axis=1)
            pieces.append(
                jnp.dot(
                    jnp.concatenate([first, second], axis=0),
                    values,
                    preferred_element_type=jnp.float32,
                )
            )
        mixture = jnp.concatenate(pieces, axis=0)
        total = mixture[:, width:]
        mixture = mixture[:, :width] * (1.0 / total)
        high = total.astype(jnp.bfloat16).astype(jnp.float32)
        stats = jnp.where(lane == 2, high, total - high)
        stats = jnp.where(lane == 0, upper, jnp.where(lane == 1, lower, stats))
        both = jnp.concatenate([mixture, stats], axis=1).astype(jnp.bfloat16)
        mixed[pl.ds(start + base, batch)] = both.reshape(batch, pairs, lines, 2 * width)
        return carry

    lax.fori_loop(0, block // batch, body, 0)


def collect_rows(index, slot_ref, mixed, outs, held):
    rows = slot_ref.shape[-1]
    clusters, _, lines, width = mixed.shape
    step = 256
    eye = iota((128, 128), 0) == iota((128, 128), 1)
    part_rows = rows // HALVES
    chunks = part_rows // 128
    sub = iota((chunks, 128), 0)

    def as_line(column):
        return jnp.sum(jnp.where(eye, column, 0.0), axis=0, keepdims=True)

    def as_column(line):
        line = line.astype(jnp.float32)
        return jnp.sum(jnp.where(eye, line, 0.0), axis=1, keepdims=True).astype(jnp.int32)

    for side in range(2):
        wide = mixed[:, pl.ds(index, 1)].reshape(clusters, lines, width).astype(jnp.float32)
        held[...] = (
            wide[:, side * RANKS : (side + 1) * RANKS]
            .reshape(clusters * RANKS, width)
            .astype(jnp.bfloat16)
        )
        for half, out_ref in enumerate(outs):
            peaks = jnp.zeros((chunks, 128), jnp.float32)
            totals = jnp.zeros((chunks, 128), jnp.float32)
            for first in range(0, part_rows, step):
                start = half * part_rows + first
                column = jnp.concatenate(
                    [
                        as_column(slot_ref[0, side : side + 1, i : i + 128])
                        for i in range(start, start + step, 128)
                    ],
                    axis=0,
                )
                picks = as_mask(iota((step, clusters * RANKS), 1) == column)
                found = jnp.dot(picks, held[...], preferred_element_type=jnp.float32)
                out_ref[side, first : first + step] = found[:, :HEAD_DIM].astype(jnp.bfloat16)
                stat = [found[:, HEAD_DIM + i : HEAD_DIM + i + 1] for i in range(4)]
                peak, total = stat[0] + stat[1], stat[2] + stat[3]
                for piece in range(step // 128):
                    here = slice(piece * 128, (piece + 1) * 128)
                    place = sub == first // 128 + piece
                    peaks = jnp.where(place, as_line(peak[here]), peaks)
                    totals = jnp.where(place, as_line(total[here]), totals)
            upper = peaks.astype(jnp.bfloat16).astype(jnp.float32)
            high = totals.astype(jnp.bfloat16).astype(jnp.float32)
            stats = jnp.concatenate([upper, peaks - upper, high, totals - high], axis=0)
            out_ref[side, part_rows : part_rows + STAT_ROWS] = stats.astype(jnp.bfloat16)


def answer_kernel(own, steps, bias_ref, own_k, own_v, pair_k, pair_v, query, slot_ref, *refs):
    *outs, mixed, held = refs
    step = pl.program_id(0)
    block = own_k.shape[0]

    @pl.when(step < steps)
    def _():
        attend_clusters(
            own, bias_ref, own_k, own_v, pair_k, pair_v, query, mixed, step * block
        )

    @pl.when(step >= steps)
    def _():
        collect_rows(step - steps, slot_ref, mixed, outs, held)


def answer(bias, own_k, own_v, pair_k, pair_v, query, slots, own, name):
    clusters, pairs, lines, width = own_k.shape
    devices, rows = slots.shape
    block = 64
    steps = clusters // block
    tall = rows // HALVES + STAT_ROWS
    last = steps - 1
    spec = pl.BlockSpec(
        (block, pairs, lines, width), lambda i: (jnp.minimum(i, last), 0, 0, 0)
    )
    return pl.pallas_call(
        functools.partial(answer_kernel, own, steps),
        grid=(steps + pairs,),
        in_specs=[pl.BlockSpec((block, 2 * pairs * lines), lambda i: (jnp.minimum(i, last), 0))]
        + [spec] * 5
        + [pl.BlockSpec((1, 2, rows), lambda i: (jnp.maximum(i - steps, 0), 0, 0))],
        out_specs=[
            pl.BlockSpec((2, tall, HEAD_DIM), lambda i: (jnp.maximum(i - steps, 0), 0, 0))
        ]
        * HALVES,
        out_shape=[jax.ShapeDtypeStruct((devices, tall, HEAD_DIM), jnp.bfloat16)] * HALVES,
        scratch_shapes=[
            pltpu.VMEM((clusters, pairs, lines, 2 * width), jnp.bfloat16),
            pltpu.VMEM((clusters * RANKS, 2 * width), jnp.bfloat16),
        ],
        compiler_params=params(),
        cost_estimate=pl.CostEstimate(
            flops=2 * devices * rows * clusters * RANKS * 2 * width,
            bytes_accessed=30_000_000,
            transcendentals=0,
        ),
        name=name,
    )(bias, own_k, own_v, pair_k, pair_v, query, slots.reshape(pairs, 2, rows))


def window_kernel(first_ref, q_ref, own_k, own_v, past_k, past_v, out_ref):
    rows = q_ref.shape[0]
    step = 256
    row = iota((step, step), 0)
    column = iota((step, step), 1)

    def run(with_past):
        for part in range(rows // step):
            query = q_ref[part * step : (part + 1) * step]
            stop = (part + 1) * step
            keys, values = own_k[:stop], own_v[:stop]
            if with_past:
                keys = jnp.concatenate([past_k[part * step :], keys], axis=0)
                values = jnp.concatenate([past_v[part * step :], values], axis=0)
            scores = contract_last(query, keys)
            span = scores.shape[1]
            pieces = []
            if with_past:
                pieces.append(jnp.where(column > row, scores[:, :step], NEGATIVE))
                pieces.append(scores[:, step : span - step])
            elif span > step:
                pieces.append(scores[:, : span - step])
            pieces.append(jnp.where(column <= row, scores[:, span - step :], NEGATIVE))
            scores = jnp.concatenate(pieces, axis=1) if len(pieces) > 1 else pieces[0]
            peak = jnp.max(scores, axis=1, keepdims=True)
            weights = jnp.exp2((scores - peak) * SCALE)
            total = jnp.sum(weights, axis=1, keepdims=True)
            mixture = jnp.dot(
                weights.astype(jnp.bfloat16), values, preferred_element_type=jnp.float32
            )
            out_ref[part * step : (part + 1) * step] = (mixture * (1.0 / total)).astype(
                jnp.bfloat16
            )

    pl.when(first_ref[0] == 0)(lambda: run(False))
    pl.when(first_ref[0] != 0)(lambda: run(True))


def window_heads(my_index, query_rows, key_rows, value_rows, past):
    rows, width = query_rows.shape
    own = pl.BlockSpec((rows, HEAD_DIM), lambda h: (0, h))
    return pl.pallas_call(
        window_kernel,
        grid=(HEADS_L,),
        in_specs=[pl.BlockSpec(memory_space=pltpu.SMEM)] + [own] * 5,
        out_specs=own,
        out_shape=jax.ShapeDtypeStruct((rows, width), jnp.bfloat16),
        compiler_params=params(),
        cost_estimate=pl.CostEstimate(
            flops=8 * HEADS_L * rows * 1280 * HEAD_DIM,
            bytes_accessed=14_000_000,
            transcendentals=0,
        ),
        name="window_heads",
    )(my_index.reshape(1), query_rows, key_rows, value_rows, *past)


def merge_kernel(count, valid_ref, *refs):
    parts, out_ref = refs[:count], refs[count]
    for device in range(out_ref.shape[0]):
        merge_rows([part.at[device] for part in parts], valid_ref, out_ref.at[device])


def merge_rows(parts, valid_ref, out_ref):
    rows = out_ref.shape[0]
    eye = iota((128, 128), 0) == iota((128, 128), 1)
    n = rows // 128
    peaks, totals = [], []
    for i, part in enumerate(parts):
        stats = part[rows : rows + STAT_ROWS].astype(jnp.float32)
        peaks.append(jnp.where(valid_ref[i] != 0, stats[:n] + stats[n : 2 * n], NEGATIVE))
        totals.append(stats[2 * n : 3 * n] + stats[3 * n : 4 * n])
    highest = functools.reduce(jnp.maximum, peaks)
    shares = [t * jnp.exp2((peak - highest) * SCALE) for t, peak in zip(totals, peaks)]
    whole = functools.reduce(jnp.add, shares)
    shares = [share / whole for share in shares]
    for piece in range(n):
        here = slice(piece * 128, (piece + 1) * 128)
        result = jnp.zeros((128, HEAD_DIM), jnp.float32)
        for part, share in zip(parts, shares):
            column = jnp.sum(
                jnp.where(eye, share[piece : piece + 1], 0.0), axis=1, keepdims=True
            )
            result = result + part[here].astype(jnp.float32) * column
        out_ref[here] = result.astype(jnp.bfloat16)


def merge(parts, valid):
    devices, tall, width = parts[0].shape
    rows = tall - STAT_ROWS
    return pl.pallas_call(
        functools.partial(merge_kernel, len(parts)),
        grid=(devices // 2,),
        in_specs=[pl.BlockSpec(memory_space=pltpu.SMEM)]
        + [pl.BlockSpec((2, tall, width), lambda i: (i, 0, 0))] * len(parts),
        out_specs=pl.BlockSpec((2, rows, width), lambda i: (i, 0, 0)),
        out_shape=jax.ShapeDtypeStruct((devices, rows, width), jnp.bfloat16),
        compiler_params=params(),
        name="merge_parts",
    )(valid, *parts)


def place_kernel(base_ref, heads_ref, out_ref):
    del base_ref
    for head in range(HEADS_R):
        out_ref[:, head * HEAD_DIM : (head + 1) * HEAD_DIM] = heads_ref[head]


def place_heads(base, heads, half):
    rows, width = base.shape
    block = 256
    steps = rows // HALVES // block
    return pl.pallas_call(
        place_kernel,
        grid=(steps,),
        in_specs=[
            pl.BlockSpec(memory_space=pl.ANY),
            pl.BlockSpec((HEADS_R, block, HEAD_DIM), lambda i: (0, i, 0)),
        ],
        out_specs=pl.BlockSpec((block, HEADS_R * HEAD_DIM), lambda i: (half * steps + i, 1)),
        out_shape=jax.ShapeDtypeStruct((rows, width), jnp.bfloat16),
        input_output_aliases={0: 0},
        compiler_params=params(),
        name="place_heads",
    )(base, heads)


def heads_kernel(in_ref, out_ref):
    for head in range(HEADS_R):
        out_ref[head] = in_ref[:, head * HEAD_DIM : (head + 1) * HEAD_DIM]


def heads_first(matrix):
    rows = matrix.shape[0]
    block = 256
    return pl.pallas_call(
        heads_kernel,
        grid=(rows // block,),
        in_specs=[pl.BlockSpec((block, HEADS_R * HEAD_DIM), lambda i: (i, 1))],
        out_specs=pl.BlockSpec((HEADS_R, block, HEAD_DIM), lambda i: (0, i, 0)),
        out_shape=jax.ShapeDtypeStruct((HEADS_R, rows, HEAD_DIM), jnp.bfloat16),
        compiler_params=params(),
        name="heads_first",
    )(matrix)


def on_device(query_rows, key_rows, value_rows, cluster_ids):
    rows = query_rows.shape[0]
    local_width = HEADS_L * HEAD_DIM
    device_count = lax.axis_size(AXES)
    my_index = lax.axis_index(AXES)
    group = HEADS_R
    planes = device_count // group
    couples = planes // 2
    plane = my_index // group
    place = my_index % group
    groups = [[group * i + j for j in range(group)] for i in range(planes)]

    def swap(array):
        return lax.all_to_all(
            array, AXES, split_axis=0, concat_axis=0, tiled=True, axis_index_groups=groups
        )

    def move(array, routes):
        pairs = [(group * a + j, group * b + j) for a, b in routes for j in range(group)]
        return lax.ppermute(array, AXES, pairs)

    def after(array, *others):
        return lax.optimization_barrier((array, *others))

    v_heads = heads_first(value_rows)
    v_heads, cluster_ids = after(v_heads, cluster_ids)
    slots, counts = rank_tokens(cluster_ids)
    facts = lax.all_gather(jnp.concatenate([slots, counts], axis=1), AXES)
    facts = lax.dynamic_index_in_dim(facts, place, 1, keepdims=False)
    facts = facts.reshape(planes, group, rows + CLUSTERS)

    def visit_routes(shift, side):
        return [(2 * j + side, 2 * (j - shift) + 1) for j in range(shift, couples)]

    pair_routes = [(2 * j, 2 * j + 1) for j in range(couples)]

    def visit(queries, shift):
        first = move(queries, visit_routes(shift, 0))
        queries, first = after(queries, first)
        return [first, move(queries, visit_routes(shift, 1))]

    def facts_of(index):
        return lax.dynamic_index_in_dim(facts, index, 0, keepdims=False)

    def bias_of(held):
        filled = jnp.arange(RANKS, dtype=jnp.int32)[None, None, :] < held.T[:, :, None]
        return jnp.where(filled, 0.0, NEGATIVE).reshape(CLUSTERS, group * RANKS)

    def visit_slots(shift):
        homes = [2 * (plane // 2 + shift) + side for side in range(2)]
        return [facts_of(jnp.minimum(home, planes - 1))[:, :rows] for home in homes]

    own_facts = facts_of(plane)
    pair_facts = facts_of(plane ^ 1)
    is_odd = plane % 2 == 1
    bias = jnp.concatenate(
        [bias_of(own_facts[:, rows:]), jnp.where(is_odd, bias_of(pair_facts[:, rows:]), NEGATIVE)],
        axis=1,
    )

    def one(slots, array, name):
        return dispatch(slots, [(array, None)], name)[0]

    own_slots, pair_slots, homes = own_facts[:, :rows], pair_facts[:, :rows], visit_slots(1)
    raw_values = move(v_heads, pair_routes)
    keys = swap(heads_first(key_rows))
    pair_keys = move(keys, pair_routes)
    q_heads, keys = after(heads_first(query_rows), keys)
    queries = swap(q_heads)
    visitors = [move(queries, visit_routes(1, 0))] if couples > 1 else []
    v_heads, queries = after(v_heads, queries)
    values = swap(v_heads)
    own_q, own_k = dispatch(own_slots, [(queries, None), (keys, None)], "dispatch_queries_keys")
    raw_values, values, own_k = after(raw_values, values, own_k)
    pair_values = swap(raw_values)
    *past, own_k = after(key_rows, value_rows, own_k)
    past = [m[:, :local_width] for m in past]
    past = [lax.ppermute(m, AXES, [(i, i + 1) for i in range(device_count - 1)]) for m in past]
    values, own_q = after(values, own_q)
    own_v = one(own_slots, values, "dispatch_values")
    if visitors:
        queries, visitors[0], own_v = after(queries, visitors[0], own_v)
        visitors.append(move(queries, visit_routes(1, 1)))
    asked = []
    if visitors:
        visitors[0], own_v = after(visitors[0], own_v)
        asked = [one(homes[0], visitors[0], "dispatch_visit")]
        pair_values, asked[0] = after(pair_values, asked[0])
    pair_k, pair_v = dispatch(
        pair_slots, [(pair_keys, None), (pair_values, None)], "dispatch_pair"
    )
    kept = (bias, own_k, own_v, pair_k, pair_v)

    parts, valid = [], [jnp.int32(1)]
    for shift in range(1, couples):
        homes = visit_slots(shift)
        if shift > 1:
            queries, parts[-1][-1] = after(queries, parts[-1][-1])
            visitors = visit(queries, shift)
            asked = [one(homes[0], visitors[0], "dispatch_visit")]
        for side in range(2):
            if side == 1:
                asked = [one(homes[1], visitors[1], "dispatch_visit")]
            found = list(answer(*kept, asked[0], homes[side], False, "answer_visit"))
            if side == 0:
                visitors[1], found[0] = after(visitors[1], found[0])
            elif shift == 1:
                own_q, found[0] = after(own_q, found[0])
            routes = [(b, a) for a, b in visit_routes(shift, side)]
            back = []
            for half in range(HALVES):
                if half and side:
                    found[half], parts[-1][-1] = after(found[half], parts[-1][-1])
                back.append(move(found[half], routes))
            parts.append(back)
            valid.append(((plane // 2 >= shift) & (plane % 2 == side)).astype(jnp.int32))
    own_found = list(answer(*kept, own_q, own_facts[:, :rows], True, "answer_own"))
    past[0], own_found[0] = after(past[0], own_found[0])
    result = window_heads(my_index, query_rows, key_rows, value_rows, past)
    valid = jnp.stack(valid)
    if parts:
        parts[-1][0], result = after(parts[-1][0], result)
    merged = []
    for half in range(HALVES):
        joined = merge([own_found[half]] + [back[half] for back in parts], valid)
        if half:
            joined, merged[-1] = after(joined, merged[-1])
        merged.append(swap(joined))
    for half in range(HALVES):
        result = place_heads(result, merged[half], half)
    return result


def solution(mesh):
    return jax.shard_map(
        on_device,
        mesh=mesh,
        in_specs=(P(AXES, None), P(AXES, None), P(AXES, None), P(None, AXES)),
        out_specs=P(AXES, None),
        check_vma=False,
    )
```

```python
import functools

import jax
import jax.numpy as jnp
from jax import lax
from jax.experimental import pallas as pl
from jax.experimental.pallas import tpu as pltpu
from jax.sharding import PartitionSpec as P

HEADS_L = 8
HEADS_R = 8
HEAD_DIM = 128
WINDOW = 1024
CLUSTERS = 256

RANKS = 8
NEGATIVE = -(2.0**100)
AXES = ("seq", "grp")
SCALE = HEAD_DIM ** (-0.5) * 1.4426950408889634
STAT_ROWS = 16
HALVES = 2
VMEM = 56 * 1024 * 1024


def params(**extra):
    return pltpu.CompilerParams(vmem_limit_bytes=VMEM, **extra)


def contract_last(a, b):
    return lax.dot_general(a, b, (((1,), (1,)), ((), ())), preferred_element_type=jnp.float32)


def iota(shape, dim):
    return lax.broadcasted_iota(jnp.int32, shape, dim)


def as_mask(condition):
    return jnp.where(condition, 1.0, 0.0).astype(jnp.bfloat16)


def rank_kernel(ids_ref, slot_ref, count_ref):
    heads, rows = ids_ref.shape
    before = as_mask(iota((rows, rows), 0) < iota((rows, rows), 1))
    ones = jnp.ones((8, rows), jnp.bfloat16)
    for head in range(heads):
        ids = ids_ref[head : head + 1, :]
        members = as_mask(iota((CLUSTERS, rows), 0) == ids)
        earlier = jnp.dot(members, before, preferred_element_type=jnp.float32)
        rank = jnp.sum(members.astype(jnp.float32) * earlier, axis=0, keepdims=True)
        slot_ref[head : head + 1, :] = ids * RANKS + rank.astype(jnp.int32)
        count_ref[head : head + 1, :] = contract_last(ones, members)[0:1].astype(jnp.int32)


def rank_tokens(cluster_ids):
    heads, rows = cluster_ids.shape
    return pl.pallas_call(
        rank_kernel,
        out_shape=(
            jax.ShapeDtypeStruct((heads, rows), jnp.int32),
            jax.ShapeDtypeStruct((heads, CLUSTERS), jnp.int32),
        ),
        compiler_params=params(),
        name="rank_tokens",
    )(cluster_ids)


def near(ids, base, step):
    here = ids - base
    return jnp.where((here >= 0) & (here < step), here, -1).astype(jnp.float32).astype(jnp.bfloat16)


def equal_mask(a, b):
    one, zero = jnp.bfloat16(1.0), jnp.bfloat16(0.0)
    return jnp.where(a == b, one, zero)


def dispatch_rows(slot_ref, read, outs):
    rows = slot_ref.shape[-1]
    fine = 256
    step = 1024
    lines = iota((fine, rows), 0).astype(jnp.float32).astype(jnp.bfloat16)

    def body(part, carry):
        base = part * step
        halves = []
        for side in range(2):
            ids = slot_ref[0, side : side + 1, :]
            picks = jnp.concatenate(
                [
                    equal_mask(
                        lines, jnp.broadcast_to(near(ids, base + i, fine), (fine, rows))
                    )
                    for i in range(0, step, fine)
                ],
                axis=0,
            )
            found = jnp.dot(picks, read(side), preferred_element_type=jnp.float32)
            halves.append(found.reshape(step // RANKS, RANKS, len(outs) * HEAD_DIM))
        joined = jnp.concatenate(halves, axis=1).astype(jnp.bfloat16)
        for i, out in enumerate(outs):
            out[pl.ds(part * (step // RANKS), step // RANKS), 0] = joined[
                :, :, i * HEAD_DIM : (i + 1) * HEAD_DIM
            ]
        return carry

    lax.fori_loop(0, CLUSTERS * RANKS // step, body, 0)


def dispatch_kernel(count, slot_ref, *refs):
    sources, outs = refs[:count], refs[count:]
    rows = slot_ref.shape[-1]

    def read(side):
        return jnp.concatenate([s[side].reshape(rows, HEAD_DIM) for s in sources], axis=1)

    dispatch_rows(slot_ref, read, outs)


def slot_block(index):
    return pl.BlockSpec((CLUSTERS, 1, 2 * RANKS, HEAD_DIM), index)


def dispatch(slots, arrays, name):
    devices, rows = slots.shape
    pairs = devices // 2
    in_specs = [pl.BlockSpec((1, 2, rows), lambda i: (i, 0, 0))]
    operands = [slots.reshape(pairs, 2, rows)]
    for array, part in arrays:
        if part is None:
            in_specs.append(pl.BlockSpec((2, rows, HEAD_DIM), lambda i: (i, 0, 0)))
        else:
            in_specs.append(
                pl.BlockSpec((2, 1, rows, HEAD_DIM), lambda i, part=part: (i, part, 0, 0))
            )
        operands.append(array)
    count = len(arrays)
    shape = (CLUSTERS, pairs, 2 * RANKS, HEAD_DIM)
    flops = 2 * devices * rows * CLUSTERS * RANKS * HEAD_DIM * count
    return pl.pallas_call(
        functools.partial(dispatch_kernel, count),
        grid=(pairs,),
        in_specs=in_specs,
        out_specs=[slot_block(lambda i: (0, i, 0, 0))] * count,
        out_shape=[jax.ShapeDtypeStruct(shape, jnp.bfloat16)] * count,
        compiler_params=params(),
        cost_estimate=pl.CostEstimate(
            flops=flops, bytes_accessed=12_000_000 * count, transcendentals=0
        ),
        name=name,
    )(*operands)


def attend_clusters(own, bias_ref, own_k, own_v, pair_k, pair_v, query, mixed, start):
    block, pairs, lines, width = own_k.shape
    slots = pairs * lines
    batch = 32
    lane = iota((slots, 2 * slots), 1)
    row = iota((slots, 2 * slots), 0)
    causal = jnp.where((lane <= row) | (lane >= slots), 0.0, NEGATIVE)
    lane = iota((1, 128), 1)
    ones = jnp.ones((4 * slots, 128), jnp.bfloat16)
    none = jnp.zeros((slots, 2 * slots), jnp.bfloat16)

    def read(ref, c):
        return ref[c].reshape(slots, width)

    def body(step, carry):
        base = step * batch
        pieces = []
        for j in range(0, batch, 2):
            here = (base + j, base + j + 1)
            keys = [read(ref, c) for c in here for ref in (own_k, pair_k)]
            asked = [read(query, c) for c in here]
            scores = contract_last(jnp.concatenate(asked, axis=0), jnp.concatenate(keys, axis=0))
            for i, c in enumerate(here):
                part = scores[i * slots : (i + 1) * slots, i * 2 * slots : (i + 1) * 2 * slots]
                part = part + bias_ref[pl.ds(c, 1), :]
                pieces.append(part + causal if own else part)
        scores = jnp.concatenate(pieces, axis=0)
        peak = jnp.max(scores, axis=1, keepdims=True)
        upper = peak.astype(jnp.bfloat16).astype(jnp.float32)
        lower = (peak - upper).astype(jnp.bfloat16).astype(jnp.float32)
        peak = upper + lower
        weights = jnp.exp2((scores - peak) * SCALE)
        weights = weights.astype(jnp.bfloat16)
        pieces = []
        for j in range(0, batch, 2):
            here = (base + j, base + j + 1)
            values = [read(ref, c) for c in here for ref in (own_v, pair_v)]
            values = jnp.concatenate([jnp.concatenate(values, axis=0), ones], axis=1)
            first = jnp.concatenate([weights[j * slots : (j + 1) * slots], none], axis=1)
            second = jnp.concatenate([none, weights[(j + 1) * slots : (j + 2) * slots]], axis=1)
            pieces.append(
                jnp.dot(
                    jnp.concatenate([first, second], axis=0),
                    values,
                    preferred_element_type=jnp.float32,
                )
            )
        mixture = jnp.concatenate(pieces, axis=0)
        total = mixture[:, width:]
        mixture = mixture[:, :width] * (1.0 / total)
        high = total.astype(jnp.bfloat16).astype(jnp.float32)
        stats = jnp.where(lane == 2, high, total - high)
        stats = jnp.where(lane == 0, upper, jnp.where(lane == 1, lower, stats))
        both = jnp.concatenate([mixture, stats], axis=1).astype(jnp.bfloat16)
        mixed[pl.ds(start + base, batch)] = both.reshape(batch, pairs, lines, 2 * width)
        return carry

    lax.fori_loop(0, block // batch, body, 0)


def collect_rows(index, slot_ref, mixed, outs, held):
    rows = slot_ref.shape[-1]
    clusters, _, lines, width = mixed.shape
    step = 256
    eye = iota((128, 128), 0) == iota((128, 128), 1)
    part_rows = rows // HALVES
    chunks = part_rows // 128
    sub = iota((chunks, 128), 0)

    def as_line(column):
        return jnp.sum(jnp.where(eye, column, 0.0), axis=0, keepdims=True)

    def as_column(line):
        line = line.astype(jnp.float32)
        return jnp.sum(jnp.where(eye, line, 0.0), axis=1, keepdims=True).astype(jnp.int32)

    for side in range(2):
        wide = mixed[:, pl.ds(index, 1)].reshape(clusters, lines, width).astype(jnp.float32)
        held[...] = (
            wide[:, side * RANKS : (side + 1) * RANKS]
            .reshape(clusters * RANKS, width)
            .astype(jnp.bfloat16)
        )
        for half, out_ref in enumerate(outs):
            peaks = jnp.zeros((chunks, 128), jnp.float32)
            totals = jnp.zeros((chunks, 128), jnp.float32)
            for first in range(0, part_rows, step):
                start = half * part_rows + first
                column = jnp.concatenate(
                    [
                        as_column(slot_ref[0, side : side + 1, i : i + 128])
                        for i in range(start, start + step, 128)
                    ],
                    axis=0,
                )
                picks = as_mask(iota((step, clusters * RANKS), 1) == column)
                found = jnp.dot(picks, held[...], preferred_element_type=jnp.float32)
                out_ref[side, first : first + step] = found[:, :HEAD_DIM].astype(jnp.bfloat16)
                stat = [found[:, HEAD_DIM + i : HEAD_DIM + i + 1] for i in range(4)]
                peak, total = stat[0] + stat[1], stat[2] + stat[3]
                for piece in range(step // 128):
                    here = slice(piece * 128, (piece + 1) * 128)
                    place = sub == first // 128 + piece
                    peaks = jnp.where(place, as_line(peak[here]), peaks)
                    totals = jnp.where(place, as_line(total[here]), totals)
            upper = peaks.astype(jnp.bfloat16).astype(jnp.float32)
            high = totals.astype(jnp.bfloat16).astype(jnp.float32)
            stats = jnp.concatenate([upper, peaks - upper, high, totals - high], axis=0)
            out_ref[side, part_rows : part_rows + STAT_ROWS] = stats.astype(jnp.bfloat16)


def answer_kernel(own, steps, bias_ref, own_k, own_v, pair_k, pair_v, query, slot_ref, *refs):
    *outs, mixed, held = refs
    step = pl.program_id(0)
    block = own_k.shape[0]

    @pl.when(step < steps)
    def _():
        attend_clusters(
            own, bias_ref, own_k, own_v, pair_k, pair_v, query, mixed, step * block
        )

    @pl.when(step >= steps)
    def _():
        collect_rows(step - steps, slot_ref, mixed, outs, held)


def answer(bias, own_k, own_v, pair_k, pair_v, query, slots, own, name):
    clusters, pairs, lines, width = own_k.shape
    devices, rows = slots.shape
    block = 64
    steps = clusters // block
    tall = rows // HALVES + STAT_ROWS
    last = steps - 1
    spec = pl.BlockSpec(
        (block, pairs, lines, width), lambda i: (jnp.minimum(i, last), 0, 0, 0)
    )
    return pl.pallas_call(
        functools.partial(answer_kernel, own, steps),
        grid=(steps + pairs,),
        in_specs=[pl.BlockSpec((block, 2 * pairs * lines), lambda i: (jnp.minimum(i, last), 0))]
        + [spec] * 5
        + [pl.BlockSpec((1, 2, rows), lambda i: (jnp.maximum(i - steps, 0), 0, 0))],
        out_specs=[
            pl.BlockSpec((2, tall, HEAD_DIM), lambda i: (jnp.maximum(i - steps, 0), 0, 0))
        ]
        * HALVES,
        out_shape=[jax.ShapeDtypeStruct((devices, tall, HEAD_DIM), jnp.bfloat16)] * HALVES,
        scratch_shapes=[
            pltpu.VMEM((clusters, pairs, lines, 2 * width), jnp.bfloat16),
            pltpu.VMEM((clusters * RANKS, 2 * width), jnp.bfloat16),
        ],
        compiler_params=params(),
        cost_estimate=pl.CostEstimate(
            flops=2 * devices * rows * clusters * RANKS * 2 * width,
            bytes_accessed=30_000_000,
            transcendentals=0,
        ),
        name=name,
    )(bias, own_k, own_v, pair_k, pair_v, query, slots.reshape(pairs, 2, rows))


def window_kernel(first_ref, q_ref, own_k, own_v, past_k, past_v, out_ref):
    rows = q_ref.shape[0]
    step = 256
    row = iota((step, step), 0)
    column = iota((step, step), 1)

    def run(with_past):
        for part in range(rows // step):
            query = q_ref[part * step : (part + 1) * step]
            stop = (part + 1) * step
            keys, values = own_k[:stop], own_v[:stop]
            if with_past:
                keys = jnp.concatenate([past_k[part * step :], keys], axis=0)
                values = jnp.concatenate([past_v[part * step :], values], axis=0)
            scores = contract_last(query, keys)
            span = scores.shape[1]
            pieces = []
            if with_past:
                pieces.append(jnp.where(column > row, scores[:, :step], NEGATIVE))
                pieces.append(scores[:, step : span - step])
            elif span > step:
                pieces.append(scores[:, : span - step])
            pieces.append(jnp.where(column <= row, scores[:, span - step :], NEGATIVE))
            scores = jnp.concatenate(pieces, axis=1) if len(pieces) > 1 else pieces[0]
            peak = jnp.max(scores, axis=1, keepdims=True)
            weights = jnp.exp2((scores - peak) * SCALE)
            total = jnp.sum(weights, axis=1, keepdims=True)
            mixture = jnp.dot(
                weights.astype(jnp.bfloat16), values, preferred_element_type=jnp.float32
            )
            out_ref[part * step : (part + 1) * step] = (mixture * (1.0 / total)).astype(
                jnp.bfloat16
            )

    pl.when(first_ref[0] == 0)(lambda: run(False))
    pl.when(first_ref[0] != 0)(lambda: run(True))


def window_heads(my_index, query_rows, key_rows, value_rows, past):
    rows, width = query_rows.shape
    own = pl.BlockSpec((rows, HEAD_DIM), lambda h: (0, h))
    return pl.pallas_call(
        window_kernel,
        grid=(HEADS_L,),
        in_specs=[pl.BlockSpec(memory_space=pltpu.SMEM)] + [own] * 5,
        out_specs=own,
        out_shape=jax.ShapeDtypeStruct((rows, width), jnp.bfloat16),
        compiler_params=params(),
        cost_estimate=pl.CostEstimate(
            flops=8 * HEADS_L * rows * 1280 * HEAD_DIM,
            bytes_accessed=14_000_000,
            transcendentals=0,
        ),
        name="window_heads",
    )(my_index.reshape(1), query_rows, key_rows, value_rows, *past)


def merge_kernel(count, valid_ref, *refs):
    parts, out_ref = refs[:count], refs[count]
    for device in range(out_ref.shape[0]):
        merge_rows([part.at[device] for part in parts], valid_ref, out_ref.at[device])


def merge_rows(parts, valid_ref, out_ref):
    rows = out_ref.shape[0]
    eye = iota((128, 128), 0) == iota((128, 128), 1)
    n = rows // 128
    peaks, totals = [], []
    for i, part in enumerate(parts):
        stats = part[rows : rows + STAT_ROWS].astype(jnp.float32)
        peaks.append(jnp.where(valid_ref[i] != 0, stats[:n] + stats[n : 2 * n], NEGATIVE))
        totals.append(stats[2 * n : 3 * n] + stats[3 * n : 4 * n])
    highest = functools.reduce(jnp.maximum, peaks)
    shares = [t * jnp.exp2((peak - highest) * SCALE) for t, peak in zip(totals, peaks)]
    whole = functools.reduce(jnp.add, shares)
    shares = [share / whole for share in shares]
    for piece in range(n):
        here = slice(piece * 128, (piece + 1) * 128)
        result = jnp.zeros((128, HEAD_DIM), jnp.float32)
        for part, share in zip(parts, shares):
            column = jnp.sum(
                jnp.where(eye, share[piece : piece + 1], 0.0), axis=1, keepdims=True
            )
            result = result + part[here].astype(jnp.float32) * column
        out_ref[here] = result.astype(jnp.bfloat16)


def merge(parts, valid):
    devices, tall, width = parts[0].shape
    rows = tall - STAT_ROWS
    return pl.pallas_call(
        functools.partial(merge_kernel, len(parts)),
        grid=(devices // 2,),
        in_specs=[pl.BlockSpec(memory_space=pltpu.SMEM)]
        + [pl.BlockSpec((2, tall, width), lambda i: (i, 0, 0))] * len(parts),
        out_specs=pl.BlockSpec((2, rows, width), lambda i: (i, 0, 0)),
        out_shape=jax.ShapeDtypeStruct((devices, rows, width), jnp.bfloat16),
        compiler_params=params(),
        name="merge_parts",
    )(valid, *parts)


def place_kernel(base_ref, heads_ref, out_ref):
    del base_ref
    for head in range(HEADS_R):
        out_ref[:, head * HEAD_DIM : (head + 1) * HEAD_DIM] = heads_ref[head]


def place_heads(base, heads, half):
    rows, width = base.shape
    block = 256
    steps = rows // HALVES // block
    return pl.pallas_call(
        place_kernel,
        grid=(steps,),
        in_specs=[
            pl.BlockSpec(memory_space=pl.ANY),
            pl.BlockSpec((HEADS_R, block, HEAD_DIM), lambda i: (0, i, 0)),
        ],
        out_specs=pl.BlockSpec((block, HEADS_R * HEAD_DIM), lambda i: (half * steps + i, 1)),
        out_shape=jax.ShapeDtypeStruct((rows, width), jnp.bfloat16),
        input_output_aliases={0: 0},
        compiler_params=params(),
        name="place_heads",
    )(base, heads)


def heads_kernel(in_ref, out_ref):
    for head in range(HEADS_R):
        out_ref[head] = in_ref[:, head * HEAD_DIM : (head + 1) * HEAD_DIM]


def heads_first(matrix):
    rows = matrix.shape[0]
    block = 256
    return pl.pallas_call(
        heads_kernel,
        grid=(rows // block,),
        in_specs=[pl.BlockSpec((block, HEADS_R * HEAD_DIM), lambda i: (i, 1))],
        out_specs=pl.BlockSpec((HEADS_R, block, HEAD_DIM), lambda i: (0, i, 0)),
        out_shape=jax.ShapeDtypeStruct((HEADS_R, rows, HEAD_DIM), jnp.bfloat16),
        compiler_params=params(),
        name="heads_first",
    )(matrix)


def on_device(query_rows, key_rows, value_rows, cluster_ids):
    rows = query_rows.shape[0]
    local_width = HEADS_L * HEAD_DIM
    device_count = lax.axis_size(AXES)
    my_index = lax.axis_index(AXES)
    group = HEADS_R
    planes = device_count // group
    couples = planes // 2
    plane = my_index // group
    place = my_index % group
    groups = [[group * i + j for j in range(group)] for i in range(planes)]

    def swap(array):
        return lax.all_to_all(
            array, AXES, split_axis=0, concat_axis=0, tiled=True, axis_index_groups=groups
        )

    def move(array, routes):
        pairs = [(group * a + j, group * b + j) for a, b in routes for j in range(group)]
        return lax.ppermute(array, AXES, pairs)

    def after(array, *others):
        return lax.optimization_barrier((array, *others))

    v_heads = heads_first(value_rows)
    v_heads, cluster_ids = after(v_heads, cluster_ids)
    slots, counts = rank_tokens(cluster_ids)
    facts = lax.all_gather(jnp.concatenate([slots, counts], axis=1), AXES)
    facts = lax.dynamic_index_in_dim(facts, place, 1, keepdims=False)
    facts = facts.reshape(planes, group, rows + CLUSTERS)

    def visit_routes(shift, side):
        return [(2 * j + side, 2 * (j - shift) + 1) for j in range(shift, couples)]

    pair_routes = [(2 * j, 2 * j + 1) for j in range(couples)]

    def visit(queries, shift):
        first = move(queries, visit_routes(shift, 0))
        queries, first = after(queries, first)
        return [first, move(queries, visit_routes(shift, 1))]

    def facts_of(index):
        return lax.dynamic_index_in_dim(facts, index, 0, keepdims=False)

    def bias_of(held):
        filled = jnp.arange(RANKS, dtype=jnp.int32)[None, None, :] < held.T[:, :, None]
        return jnp.where(filled, 0.0, NEGATIVE).reshape(CLUSTERS, group * RANKS)

    def visit_slots(shift):
        homes = [2 * (plane // 2 + shift) + side for side in range(2)]
        return [facts_of(jnp.minimum(home, planes - 1))[:, :rows] for home in homes]

    own_facts = facts_of(plane)
    pair_facts = facts_of(plane ^ 1)
    is_odd = plane % 2 == 1
    bias = jnp.concatenate(
        [bias_of(own_facts[:, rows:]), jnp.where(is_odd, bias_of(pair_facts[:, rows:]), NEGATIVE)],
        axis=1,
    )

    def one(slots, array, name):
        return dispatch(slots, [(array, None)], name)[0]

    own_slots, pair_slots, homes = own_facts[:, :rows], pair_facts[:, :rows], visit_slots(1)
    raw_values = move(v_heads, pair_routes)
    keys = swap(heads_first(key_rows))
    pair_keys = move(keys, pair_routes)
    q_heads, keys = after(heads_first(query_rows), keys)
    queries = swap(q_heads)
    visitors = [move(queries, visit_routes(1, 0))] if couples > 1 else []
    v_heads, queries = after(v_heads, queries)
    values = swap(v_heads)
    own_q, own_k = dispatch(own_slots, [(queries, None), (keys, None)], "dispatch_queries_keys")
    raw_values, values, own_k = after(raw_values, values, own_k)
    pair_values = swap(raw_values)
    *past, own_k = after(key_rows, value_rows, own_k)
    past = [m[:, :local_width] for m in past]
    onward = [(i, i + 1) for i in range(device_count - 1)]
    past[0] = lax.ppermute(past[0], AXES, onward)
    past[1], past[0] = after(past[1], past[0])
    past[1] = lax.ppermute(past[1], AXES, onward)
    values, own_q = after(values, own_q)
    own_v = one(own_slots, values, "dispatch_values")
    if visitors:
        queries, visitors[0], own_v = after(queries, visitors[0], own_v)
        visitors.append(move(queries, visit_routes(1, 1)))
    asked = []
    if visitors:
        visitors[0], own_v = after(visitors[0], own_v)
        asked = [one(homes[0], visitors[0], "dispatch_visit")]
        pair_values, asked[0] = after(pair_values, asked[0])
    pair_k, pair_v = dispatch(
        pair_slots, [(pair_keys, None), (pair_values, None)], "dispatch_pair"
    )
    kept = (bias, own_k, own_v, pair_k, pair_v)

    parts, valid = [], [jnp.int32(1)]
    for shift in range(1, couples):
        homes = visit_slots(shift)
        if shift > 1:
            queries, parts[-1][-1] = after(queries, parts[-1][-1])
            visitors = visit(queries, shift)
            asked = [one(homes[0], visitors[0], "dispatch_visit")]
        for side in range(2):
            if side == 1:
                asked = [one(homes[1], visitors[1], "dispatch_visit")]
            found = list(answer(*kept, asked[0], homes[side], False, "answer_visit"))
            if side == 0:
                visitors[1], found[0] = after(visitors[1], found[0])
            elif shift == 1:
                own_q, found[0] = after(own_q, found[0])
            routes = [(b, a) for a, b in visit_routes(shift, side)]
            back = []
            for half in range(HALVES):
                if half and side:
                    found[half], parts[-1][-1] = after(found[half], parts[-1][-1])
                back.append(move(found[half], routes))
            parts.append(back)
            valid.append(((plane // 2 >= shift) & (plane % 2 == side)).astype(jnp.int32))
    own_found = list(answer(*kept, own_q, own_facts[:, :rows], True, "answer_own"))
    past[0], own_found[0] = after(past[0], own_found[0])
    result = window_heads(my_index, query_rows, key_rows, value_rows, past)
    valid = jnp.stack(valid)
    if parts:
        parts[-1][0], result = after(parts[-1][0], result)
    merged = []
    for half in range(HALVES):
        joined = merge([own_found[half]] + [back[half] for back in parts], valid)
        if half:
            joined, merged[-1] = after(joined, merged[-1])
        merged.append(swap(joined))
    for half in range(HALVES):
        result = place_heads(result, merged[half], half)
    return result


def solution(mesh):
    return jax.shard_map(
        on_device,
        mesh=mesh,
        in_specs=(P(AXES, None), P(AXES, None), P(AXES, None), P(None, AXES)),
        out_specs=P(AXES, None),
        check_vma=False,
    )
```
